256 devices in a mesh: seq: 16 (over y, x_hi, core), chan: 16 (over x_lo, z).
Axes of the slice: x: 4 (x_hi: 2, x_lo: 2; x = x_hi * 2 + x_lo), y: 4, z: 8, core: 2. Of those that a mesh axis runs over, the one named last changes fastest.
Arguments:
- tokens: bfloat16 [16384, 4096], P('seq', 'chan'), may hold values from -6 to 6
- in_weight: bfloat16 [3, 4096, 2048], P(None, None, 'chan'), may hold values from -0.09375 to 0.09375
- conv_weight: float32 [3, 3, 2048], P(None, None, 'chan'), may hold values from -3 to 3
- spectrum: float32 [2, 2048, 32, 1024], P(None, 'chan', 'seq'), may hold values from -6 to 6
- skip: float32 [2048], P('chan'), may hold values from -4 to 4
- out_weight: bfloat16 [2048, 4096], P('chan'), may hold values from -0.125 to 0.125
Outputs:
- mixed: bfloat16 [16384, 4096], P('seq', 'chan')
The draws below stay inside these ranges and needn't reach their ends.
All inputs are finite; a program needn't handle non-finite values.
Results may differ from the reference program's by a relative error of at most 0.03.
Values may be sent and summed in bfloat16 or wider, within the bound.
A program may use at most 192 MiB of HBM per device.

```python
import jax
import jax.numpy as jnp
from jax import lax

D = 4096
C = 2048
TAPS = 3
TOK_DEV = 1024
TOKENS = 16384
KB = 32
NFFT = 32768
N_CHAN = 16


def levels(rng, extent, cuts, low, largest):
    level, own = 1.0, jax.random.fold_in(rng, 6)
    for dim, shards_of in cuts:
        heights = jnp.exp(jax.random.uniform(jax.random.fold_in(own, dim), (shards_of,), jnp.float32, low / len(cuts), largest / len(cuts)))
        level = level * jnp.repeat(heights, extent[dim] // shards_of).reshape([-1 if axis == dim else 1 for axis in range(len(extent))])
    return level


def gaussian(rng, dims, scale, most, cuts=(), dtype=jnp.bfloat16):
    drawn = jax.random.normal(rng, dims, jnp.float32) * scale
    if len(cuts) > 0:
        drawn = levels(rng, dims, cuts, -0.22, 0.18) * drawn
    return jnp.clip(drawn, min=-most, max=most).astype(dtype)


def setup_inputs(seed: int = 0) -> dict:
    streams_of = jax.random.split(jax.random.key(seed), 7)
    tokens = gaussian(streams_of[0], (TOKENS, D), 1.0, 6.0, ((0, 16), (1, 16)))
    in_weight = gaussian(streams_of[1], (3, D, C), D ** -0.5, 0.09375, ((2, 16),))
    conv_weight = gaussian(streams_of[2], (TAPS, 3, C), 0.6, 3.0, ((2, 16),), jnp.float32)
    spectrum = gaussian(streams_of[3], (2, C, KB, TOK_DEV), 1.0, 6.0, ((1, 16), (2, 16)), jnp.float32)
    skip = gaussian(streams_of[4], (C,), 1.0, 4.0, ((0, 16),), jnp.float32)
    out_weight = gaussian(streams_of[5], (C, D), C ** -0.5, 0.125, ((0, 16),))
    return dict(tokens=tokens, in_weight=in_weight, conv_weight=conv_weight, spectrum=spectrum, skip=skip, out_weight=out_weight)


def reference(tokens, in_weight, conv_weight, spectrum, skip, out_weight):
    projected = jnp.einsum("td,pdc->pct", tokens.astype(jnp.float32), in_weight.astype(jnp.float32)).astype(jnp.bfloat16)
    seq_length = projected.shape[2]
    margin = TAPS - 1
    padded = jnp.pad(projected.astype(jnp.float32), ((0, 0), (0, 0), (margin, 0)))
    filtered = conv_weight[0][:, :, None] * padded[:, :, margin:margin + seq_length]
    for tap_index in range(1, TAPS):
        filtered = filtered + conv_weight[tap_index][:, :, None] * padded[:, :, margin - tap_index:margin - tap_index + seq_length]
    query_rows = filtered[0]
    signal = (filtered[1] * filtered[2]).astype(jnp.bfloat16)
    response = lax.complex(spectrum[0], spectrum[1]).transpose(0, 2, 1).reshape(C, NFFT)
    width_block = min(C, 256)
    signal_blocks = signal.astype(jnp.float32).reshape(C // width_block, width_block, seq_length)
    response_blocks = response.reshape(C // width_block, width_block, NFFT)

    def convolve(paired):
        values, filter_block = paired
        extended = jnp.pad(values, ((0, 0), (0, NFFT - seq_length)))
        frequencies = jnp.fft.fft(extended, axis=1)
        return jnp.real(jnp.fft.ifft(frequencies * filter_block, axis=1))[:, :seq_length]

    longconv = lax.map(convolve, (signal_blocks, response_blocks)).reshape(C, seq_length)
    gated = (query_rows * (longconv + skip[:, None] * signal.astype(jnp.float32))).astype(jnp.bfloat16)
    group_rows = C // N_CHAN
    gated_groups = gated.reshape(N_CHAN, group_rows, seq_length)
    weight_groups = out_weight.reshape(N_CHAN, group_rows, D)

    def add_group(running, paired):
        gated_part, weight_part = paired
        partial_out = jnp.dot(gated_part.T, weight_part, preferred_element_type=jnp.float32).astype(jnp.bfloat16)
        partial_out = lax.optimization_barrier(partial_out)
        return running + partial_out.astype(jnp.float32), None

    total, unused = lax.scan(add_group, jnp.zeros((seq_length, D), jnp.float32), (gated_groups, weight_groups))
    return total.astype(jnp.bfloat16)
```

```python
import math

import jax
import jax.numpy as jnp
import numpy as np
from jax import lax
from jax.experimental import pallas as pl
from jax.experimental.pallas import tpu as pltpu
from jax.sharding import PartitionSpec as P

MESH = pl.DeviceIdType.MESH
LANES = 128
SUB = 8
BF16 = jnp.bfloat16
F32 = jnp.float32


class Plan:
    def __init__(self, ns, nch, n_y, x_hi, tok, ds, ec):
        self.ns, self.nch, self.nz, self.n_y, self.x_hi = ns, nch, nch // 2, n_y, x_hi
        self.tok, self.half, self.ds, self.ec = tok, tok // 2, ds, ec
        self.cpd = SUB * ns
        self.d, self.e = nch * ds, nch * ec
        self.nhi = ns * tok // LANES
        self.ka = 2 * self.nhi
        self.nfft = 2 * ns * tok
        self.k1 = 2 * ns
        self.m = self.ka // self.k1
        self.k2 = self.m * LANES
        self.blocks = self.half // LANES
        self.rows = self.blocks * SUB
        self.piece = self.cpd // (2 * n_y)


def tables(plan):
    k1l, m, s = np.meshgrid(np.arange(2), np.arange(plan.m), np.arange(plan.ns), indexing="ij")
    ka = (2 * s + k1l + plan.k1 * m).reshape(-1).astype(np.int64)
    nhi = np.arange(plan.nhi, dtype=np.int64)
    lane = np.arange(LANES, dtype=np.int64)

    def angle(a, b, mod):
        return (a[:, None] * b[None, :] % mod) * (2.0 * math.pi / mod)

    left = angle(ka, nhi, plan.ka)
    f1 = np.concatenate([np.cos(left), -np.sin(left)], axis=0)
    g1 = np.concatenate([np.cos(left.T), -np.sin(left.T)], axis=1) / plan.nfft
    turn = angle(ka, lane, plan.nfft)
    tw = np.stack([np.cos(turn), -np.sin(turn)])
    right = angle(lane, lane, LANES)
    c, sn = np.cos(right), np.sin(right)
    f2 = np.block([[c, -sn], [sn, c]])
    g2 = np.block([[c, sn], [-sn, c]])
    order = np.zeros((plan.k2, plan.k2), np.float32)
    k2 = np.arange(plan.k2)
    order[k2, (k2 % plan.m) * LANES + k2 // plan.m] = 1.0
    as_bf16 = lambda a: jnp.asarray(a.astype(np.float32).astype(BF16))
    return (as_bf16(f1), as_bf16(g1), jnp.asarray(tw.astype(np.float32)), as_bf16(f2), as_bf16(g2), as_bf16(order))


def kernel(
    plan, tokens, in_w, spec, out_w, f1_h, g1_h, tw_h, f2_h, g2_h, ord_h, conv_w, skip_w, out,
    w_own, w_far, tok_v, acc, spec_v, ord_v, spec_s, spec_r, spec_f, proj_s, proj_r, proj_f,
    gate_f, gate_s, gate_r, gate_a, ow, o_acc, o_own, o_far, f1, g1, tw, f2, g2,
    load_sem, ring_send, ring_recv, ring2_send, ring2_recv, x_sem, w_send, w_recv,
    a2a_send, a2a_recv, ow_send, ow_recv, out_sem,
):
    ns, nz, nch, n_y, half, ds, ec = plan.ns, plan.nz, plan.nch, plan.n_y, plan.half, plan.ds, plan.ec
    s, c = lax.axis_index("seq"), lax.axis_index("chan")
    core, xh, y = lax.rem(s, 2), lax.rem(s // 2, plan.x_hi), s // (2 * plan.x_hi)
    xl, z = c // nz, lax.rem(c, nz)
    other = 1 - xl
    partner = other * nz + z

    def seq_of(y_, xh_, core_):
        return (y_ * plan.x_hi + xh_) * 2 + core_

    def remote(src, dst, ss, rs, seq, chan):
        return pltpu.make_async_remote_copy(
            src_ref=src, dst_ref=dst, send_sem=ss, recv_sem=rs,
            device_id={"seq": seq, "chan": chan}, device_id_type=MESH,
        )

    def arrived(ref, sem):
        pltpu.make_async_copy(ref, ref, sem).wait()

    loads = [
        (tokens.at[pl.ds(xl * half, half), :], tok_v.at[c]), (in_w, w_own), (spec, spec_v), (ord_h, ord_v),
        (f1_h, f1), (g1_h, g1), (tw_h, tw), (f2_h, f2), (g2_h, g2),
    ]
    loads = [pltpu.make_async_copy(a, b, load_sem.at[i]) for i, (a, b) in enumerate(loads)]

    me = xl * ns + s
    peers = 2 * ns
    bar = pltpu.get_barrier_semaphore()

    def greet_plane(d, carry):
        q = lax.rem(me + d, peers)
        pl.semaphore_signal(bar, inc=1, device_id={"seq": lax.rem(q, ns), "chan": (q // ns) * nz + z}, device_id_type=MESH)
        return carry

    def greet_line(d, carry):
        zz = lax.rem(z + d, nz)
        for g in range(2):
            pl.semaphore_signal(bar, inc=1, device_id={"seq": s, "chan": g * nz + zz}, device_id_type=MESH)
        return carry

    lax.fori_loop(1, peers, greet_plane, 0)
    lax.fori_loop(1, nz, greet_line, 0)
    for cp in loads:
        cp.start()
    pl.semaphore_wait(bar, peers - 1 + 2 * (nz - 1))

    hops = nz // 2
    reach = {(0, 0): hops, (1, 0): nz - 1 - hops, (0, 1): nz - 1 - hops, (1, 1): hops}

    def slot(grp, way, k):
        zz = lax.rem(z + nz - k, nz) if way == 0 else lax.rem(z + k, nz)
        return (xl if grp == 0 else other) * nz + zz

    def ring_copy(buf, send, recv, way, grp, k, src=None):
        to = lax.rem(z + 1, nz) if way == 0 else lax.rem(z + nz - 1, nz)
        at = slot(grp, way, k)
        return remote(buf.at[at] if src is None else src, buf.at[at], send.at[way, grp, k], recv.at[way, grp, k], s, xl * nz + to)

    sent = []

    def go(cp):
        cp.start()
        sent.append(cp)

    def ring_start(buf, send, recv, grp, src=None):
        for way in range(2):
            if reach[way, grp] > 0:
                go(ring_copy(buf, send, recv, way, grp, 0, src))

    def ring_step(buf, send, recv, grp, k):
        got = []
        for way in range(2):
            if k <= reach[way, grp]:
                at = slot(grp, way, k)
                arrived(buf.at[at], recv.at[way, grp, k - 1])
                if k < reach[way, grp]:
                    go(ring_copy(buf, send, recv, way, grp, k))
                got.append(at)
        return got

    mine = tokens.at[pl.ds(xl * half, half), :]
    x_copy = remote(tokens.at[pl.ds(other * half, half), :], tok_v.at[c], x_sem.at[0], x_sem.at[1], s, partner)
    x_copy.start()
    sent.append(x_copy)
    ring_start(tok_v, ring_send, ring_recv, 0, mine)

    quarter = plan.d // 4
    right_xh = lax.rem(xh + xl, plan.x_hi)
    left_xh = lax.rem(xh + plan.x_hi - 1 + xl, plan.x_hi)

    def w_rows(q):
        return pl.ds(pl.multiple_of(q * quarter, quarter), quarter)

    for i, xh_ in ((0, right_xh), (1, left_xh)):
        q = 2 * core + i
        go(remote(in_w.at[:, w_rows(q), :], w_far.at[:, w_rows(q), :], w_send.at[i], w_recv.at[i], seq_of(y, xh_, core), partner))

    loads[2].wait()
    loads[3].wait()

    step = min(plan.cpd * 2, 128)
    for p in range(2):
        for r0 in range(0, 2 * plan.cpd, step):
            turned = jnp.dot(spec_v[p, r0 : r0 + step, :], ord_v[...], preferred_element_type=F32).astype(BF16)
            for m in range(plan.m):
                spec_s[r0 // 16 : (r0 + step) // 16, p, m] = turned[:, m * LANES : (m + 1) * LANES].reshape(step // 16, 16, LANES)

    def send_spec(d, carry):
        q = lax.rem(s + d, ns)
        remote(spec_s.at[q], spec_r.at[s], a2a_send.at[0], a2a_recv.at[0], q, c).start()
        return carry

    lax.fori_loop(1, ns, send_spec, 0)
    spec_own = pltpu.make_async_copy(spec_s.at[s], spec_r.at[s], load_sem.at[9])
    spec_own.start()

    def project(grps, at, first=False):
        tk = tok_v[at]
        rows = pl.ds(pl.multiple_of(at * ds, ds), ds)
        for g in grps:
            w = w_own if g == 0 else w_far
            for p in range(3):
                part = lax.dot_general(w[p, rows, :], tk, (((0,), (1,)), ((), ())), preferred_element_type=F32)
                if first:
                    acc[g, p] = part
                else:
                    acc[g, p] = acc[g, p] + part

    loads[0].wait()
    loads[1].wait()
    project([0], c, True)
    arrived(tok_v.at[partner], x_sem.at[1])
    ring_start(tok_v, ring_send, ring_recv, 1)
    project([0], partner)
    far_ready = False
    for k in range(1, hops + 1):
        last = k == max(hops - 1, 1)
        got = ring_step(tok_v, ring_send, ring_recv, 0, k)
        if far_ready:
            for at in got:
                project([0, 1], at)
        elif not last:
            for at in got:
                project([0], at)
        more = ring_step(tok_v, ring_send, ring_recv, 1, k)
        if far_ready:
            for at in more:
                project([0, 1], at)
        elif not last:
            for at in more:
                project([0], at)
        else:
            side = pl.ds(pl.multiple_of(core * 2 * quarter, 2 * quarter), 2 * quarter)
            for i in range(2):
                arrived(w_far.at[:, w_rows(2 * core + i), :], w_recv.at[i])
            go(remote(w_far.at[:, side, :], w_far.at[:, side, :], w_send.at[2], w_recv.at[2], seq_of(y, xh, 1 - core), c))
            for at in got + more:
                project([0], at)
            away = pl.ds(pl.multiple_of((1 - core) * 2 * quarter, 2 * quarter), 2 * quarter)
            arrived(w_far.at[:, away, :], w_recv.at[2])
            far_ready = True
            project([1], c, True)
            project([1], partner)

            def catch_up(i, carry):
                for grp in range(2):
                    project([1], slot(grp, 1, i))
                return carry

            if k < hops:
                lax.fori_loop(1, k + 1, catch_up, 0)
                lax.fori_loop(nz - k, nz, catch_up, 0)
            else:
                lax.fori_loop(1, nz, catch_up, 0)

    row = pl.ds(pl.multiple_of((core * n_y + y) * plan.piece, plan.piece), plan.piece)

    def cols(b):
        return pl.ds(pl.multiple_of(b * ec, ec), ec)

    def ow_first(d, carry):
        to = lax.rem(c + d, nch)
        for g in range(2):
            remote(
                out_w.at[row, cols(g * nz + lax.rem(to, nz))], ow.at[c, row, g * ec : (g + 1) * ec],
                ow_send.at[0], ow_recv.at[0], s, to,
            ).start()
        return carry

    ow_own = [
        pltpu.make_async_copy(out_w.at[row, cols(g * nz + z)], ow.at[c, row, g * ec : (g + 1) * ec], load_sem.at[10 + g])
        for g in range(2)
    ]

    for g in range(2):
        q0 = jnp.where(g == 0, xl, other) * ns
        for p in range(3):
            for j in range(plan.blocks // 2):
                pair = [
                    acc[g, p, :, (2 * j + i) * LANES : (2 * j + i + 1) * LANES].reshape(ns, SUB, LANES) for i in range(2)
                ]
                proj_s[pl.ds(q0, ns), p, j] = jnp.concatenate(pair, axis=1).astype(BF16)

    here = 2 * s + xl

    def send_proj(d, carry):
        q = lax.rem(me + d, peers)
        remote(proj_s.at[q], proj_r.at[here], a2a_send.at[1], a2a_recv.at[1], lax.rem(q, ns), (q // ns) * nz + z).start()
        return carry

    lax.fori_loop(1, peers, send_proj, 0)
    proj_own = pltpu.make_async_copy(proj_s.at[me], proj_r.at[here], load_sem.at[12])
    proj_own.start()
    lax.fori_loop(1, nch, ow_first, 0)
    for cp in ow_own:
        cp.start()

    spec_own.wait()
    arrived(spec_r.at[0 : ns - 1], a2a_recv.at[0])

    def lay(i, carry):
        for p in range(2):
            for m in range(plan.m):
                spec_f[p, pl.ds(pl.multiple_of((m * ns + i) * 16, 16), 16), :] = spec_r[i, p, m].astype(F32)
        return carry

    lax.fori_loop(0, ns, lay, 0)
    for cp in loads[4:]:
        cp.wait()

    proj_own.wait()
    arrived(proj_r.at[0 : peers - 1], a2a_recv.at[1])
    for cp in ow_own:
        cp.wait()
    arrived(ow.at[0 : nch - 1, row, :], ow_recv.at[0])
    for dy in range(1, n_y):
        go(remote(ow.at[:, row, :], ow.at[:, row, :], ow_send.at[dy], ow_recv.at[dy], seq_of(lax.rem(y + dy, n_y), xh, core), c))

    for p in range(3):
        proj_f[p] = proj_r[:, p].astype(F32).reshape(plan.nhi * SUB, LANES)

    lane = lax.broadcasted_iota(jnp.int32, (plan.nhi, LANES), 1)
    posn = lane + LANES * lax.broadcasted_iota(jnp.int32, (plan.nhi, LANES), 0)

    def behind(x, by):
        turned = pltpu.roll(x, by, 1)
        both = jnp.where(lane < by, pltpu.roll(turned, 1, 0), turned)
        return jnp.where(posn < by, 0.0, both)

    def transform(ch, carry):
        chan = s * SUB + ch
        parts = []
        for p in range(3):
            x = proj_f[p, pl.ds(ch, plan.nhi, stride=SUB), :]
            f = conv_w[0, p, chan] * x
            for j in range(1, 3):
                f = f + conv_w[j, p, chan] * behind(x, j)
            parts.append(f)
        query, signal = parts[0], (parts[1] * parts[2]).astype(BF16)
        a = jnp.dot(f1[...], signal, preferred_element_type=F32)
        ar, ai = a[: plan.ka], a[plan.ka :]
        tr, ti = tw[0], tw[1]
        yy = jnp.concatenate([(ar * tr - ai * ti).astype(BF16), (ar * ti + ai * tr).astype(BF16)], axis=1)
        zz = jnp.dot(yy, f2[...], preferred_element_type=F32)
        zr, zi = zz[:, :LANES], zz[:, LANES:]
        h = []
        for p in range(2):
            h.append(jnp.concatenate(
                [spec_f[p, pl.ds(2 * ch + k, plan.m * ns, stride=16), :] for k in range(2)], axis=0))
        pp = jnp.concatenate([(zr * h[0] - zi * h[1]).astype(BF16), (zr * h[1] + zi * h[0]).astype(BF16)], axis=1)
        u = jnp.dot(pp, g2[...], preferred_element_type=F32)
        ur, ui = u[:, :LANES], u[:, LANES:]
        v = jnp.concatenate([(ur * tr + ui * ti).astype(BF16), (ui * tr - ur * ti).astype(BF16)], axis=0)
        longconv = jnp.dot(g1[...], v, preferred_element_type=F32)
        gate_f[pl.ds(ch, plan.nhi, stride=SUB), :] = query * (longconv + skip_w[chan] * signal.astype(F32))
        return carry

    lax.fori_loop(0, SUB, transform, 0, unroll=2)
    gate_s[...] = gate_f[...].astype(BF16).reshape(peers, plan.rows, LANES)

    def send_gate(d, carry):
        q = lax.rem(here + d, peers)
        remote(gate_s.at[q], gate_r.at[me], a2a_send.at[2], a2a_recv.at[2], q // 2, lax.rem(q, 2) * nz + z).start()
        return carry

    lax.fori_loop(1, peers, send_gate, 0)
    gate_own = pltpu.make_async_copy(gate_s.at[here], gate_r.at[me], load_sem.at[13])
    gate_own.start()
    for dy in range(1, n_y):
        yy = lax.rem(y + n_y - dy, n_y)
        piece = pl.ds(pl.multiple_of((core * n_y + yy) * plan.piece, plan.piece), plan.piece)
        arrived(ow.at[:, piece, :], ow_recv.at[dy])
    wide = plan.piece * n_y
    side = pl.ds(pl.multiple_of(core * wide, wide), wide)
    go(remote(ow.at[:, side, :], ow.at[:, side, :], ow_send.at[n_y], ow_recv.at[n_y], seq_of(y, xh, 1 - core), c))

    gate_own.wait()
    arrived(gate_r.at[0 : peers - 1], a2a_recv.at[2])
    for grp in range(2):
        g = xl if grp == 0 else other
        for j in range(plan.blocks // 2):
            pair = gate_r[pl.ds(g * ns, ns), 16 * j : 16 * (j + 1), :].astype(F32)
            for i in range(2):
                block = pair[:, SUB * i : SUB * (i + 1), :].reshape(plan.cpd, LANES)
                at = (2 * j + i) * LANES
                gate_a[g * nz + z, at : at + LANES, :] = block.T.astype(BF16)
        ring_start(gate_a, ring2_send, ring2_recv, grp)
    away = pl.ds(pl.multiple_of((1 - core) * wide, wide), wide)
    arrived(ow.at[:, away, :], ow_recv.at[n_y])

    def mix(at):
        o_acc[...] = o_acc[...] + jnp.dot(gate_a[at], ow[at], preferred_element_type=F32)

    o_acc[...] = jnp.dot(gate_a[c], ow[c], preferred_element_type=F32)
    mix(partner)
    for k in range(1, hops + 1):
        for grp in range(2):
            for at in ring_step(gate_a, ring2_send, ring2_recv, grp, k):
                mix(at)

    mixed = [o_acc[:, g * ec : (g + 1) * ec].astype(BF16) for g in range(2)]
    o_far[...] = jnp.where(xl == 0, mixed[1], mixed[0])
    mine = pl.ds(pl.multiple_of(xl * half, half), half)
    theirs = pl.ds(pl.multiple_of(other * half, half), half)
    go(remote(o_far, out.at[mine, :], out_sem.at[0], out_sem.at[1], s, partner))
    o_own[...] = jnp.where(xl == 0, mixed[0], mixed[1])
    keep = pltpu.make_async_copy(o_own, out.at[mine, :], out_sem.at[2])
    keep.start()

    for cp in sent:
        cp.wait_send()
    arrived(spec_s.at[0 : ns - 1], a2a_send.at[0])
    arrived(proj_s.at[0 : peers - 1], a2a_send.at[1])
    arrived(gate_s.at[0 : peers - 1], a2a_send.at[2])
    arrived(ow.at[0 : nch - 1, row, :], ow_send.at[0])
    keep.wait()
    arrived(out.at[theirs, :], out_sem.at[1])


def make(plan):
    consts = tables(plan)

    def shards(tokens, in_weight, conv_weight, spectrum, skip, out_weight):
        spec = spectrum.reshape(2, 2 * plan.cpd, plan.k2).astype(BF16)
        ns, peers, cpd = plan.ns, 2 * plan.ns, plan.cpd
        hops = plan.nz // 2
        vm = pltpu.VMEM
        dma = pltpu.SemaphoreType.DMA
        anywhere = pl.BlockSpec(memory_space=pl.ANY)
        scalars = pl.BlockSpec(memory_space=pltpu.SMEM)
        return pl.pallas_call(
            lambda *refs: kernel(plan, *refs),
            out_shape=jax.ShapeDtypeStruct((plan.tok, plan.ec), BF16),
            in_specs=[anywhere] * 10 + [scalars] * 2,
            out_specs=anywhere,
            scratch_shapes=[
                vm((3, plan.d, cpd), BF16), vm((3, plan.d, cpd), BF16),
                vm((plan.nch, plan.half, plan.ds), BF16),
                vm((2, 3, cpd, plan.half), F32),
                vm((2, 2 * cpd, plan.k2), BF16), vm((plan.k2, plan.k2), BF16),
                vm((ns, 2, plan.m, 16, LANES), BF16), vm((ns, 2, plan.m, 16, LANES), BF16),
                vm((2, plan.m * ns * 16, LANES), F32),
                vm((peers, 3, plan.blocks // 2, 16, LANES), BF16),
                vm((peers, 3, plan.blocks // 2, 16, LANES), BF16),
                vm((3, plan.nhi * SUB, LANES), F32),
                vm((plan.nhi * SUB, LANES), F32),
                vm((peers, plan.rows, LANES), BF16), vm((peers, plan.rows, LANES), BF16),
                vm((plan.nch, plan.half, cpd), BF16),
                vm((plan.nch, cpd, 2 * plan.ec), BF16),
                vm((plan.half, 2 * plan.ec), F32),
                vm((plan.half, plan.ec), BF16), vm((plan.half, plan.ec), BF16),
                vm((2 * plan.ka, plan.nhi), BF16), vm((plan.nhi, 2 * plan.ka), BF16),
                vm((2, plan.ka, LANES), F32),
                vm((2 * LANES, 2 * LANES), BF16), vm((2 * LANES, 2 * LANES), BF16),
                dma((14,)), dma((2, 2, hops)), dma((2, 2, hops)), dma((2, 2, hops)), dma((2, 2, hops)),
                dma((2,)), dma((3,)), dma((3,)), dma((3,)), dma((3,)),
                dma((plan.n_y + 1,)), dma((plan.n_y + 1,)), dma((3,)),
            ],
            compiler_params=pltpu.CompilerParams(
                collective_id=0, has_side_effects=True, vmem_limit_bytes=56 * 1024 * 1024
            ),
            name="hyena",
        )(tokens, in_weight, spec, out_weight, *consts, conv_weight, skip)

    return shards


def on_mesh(mesh, plan):
    placed = (
        P("seq", "chan"),
        P(None, None, "chan"),
        P(None, None, "chan"),
        P(None, "chan", "seq", None),
        P("chan"),
        P("chan", None),
    )
    return jax.shard_map(make(plan), mesh=mesh, in_specs=placed, out_specs=P("seq", "chan"), check_vma=False)


def solution(mesh):
    return on_mesh(mesh, Plan(ns=16, nch=16, n_y=4, x_hi=2, tok=1024, ds=256, ec=256))
```

```python
import math

import jax
import jax.numpy as jnp
import numpy as np
from jax import lax
from jax.experimental import pallas as pl
from jax.experimental.pallas import tpu as pltpu
from jax.sharding import PartitionSpec as P

MESH = pl.DeviceIdType.MESH
LANES = 128
SUB = 8
BF16 = jnp.bfloat16
F32 = jnp.float32


class Plan:
    def __init__(self, ns, nch, n_y, x_hi, tok, ds, ec):
        self.ns, self.nch, self.nz, self.n_y, self.x_hi = ns, nch, nch // 2, n_y, x_hi
        self.tok, self.half, self.ds, self.ec = tok, tok // 2, ds, ec
        self.cpd = SUB * ns
        self.d, self.e = nch * ds, nch * ec
        self.nhi = ns * tok // LANES
        self.ka = 2 * self.nhi
        self.nfft = 2 * ns * tok
        self.k1 = 2 * ns
        self.m = self.ka // self.k1
        self.k2 = self.m * LANES
        self.blocks = self.half // LANES
        self.rows = self.blocks * SUB
        self.piece = self.cpd // (2 * n_y)


def tables(plan):
    m, s, k1l = np.meshgrid(np.arange(plan.m), np.arange(plan.ns), np.arange(2), indexing="ij")
    ka = (2 * s + k1l + plan.k1 * m).reshape(-1).astype(np.int64)
    nhi = np.arange(plan.nhi, dtype=np.int64)
    lane = np.arange(LANES, dtype=np.int64)

    def angle(a, b, mod):
        return (a[:, None] * b[None, :] % mod) * (2.0 * math.pi / mod)

    left = angle(ka, nhi, plan.ka)
    f1 = np.concatenate([np.cos(left), -np.sin(left)], axis=0)
    g1 = np.concatenate([np.cos(left.T), -np.sin(left.T)], axis=1) / plan.nfft
    turn = angle(ka, lane, plan.nfft)
    tw = np.stack([np.cos(turn), -np.sin(turn)])
    right = angle(lane, lane, LANES)
    c, sn = np.cos(right), np.sin(right)
    f2 = np.block([[c, -sn], [sn, c]])
    g2 = np.block([[c, sn], [-sn, c]])
    order = np.zeros((plan.k2, plan.k2), np.float32)
    k2 = np.arange(plan.k2)
    order[k2, (k2 % plan.m) * LANES + k2 // plan.m] = 1.0
    as_bf16 = lambda a: jnp.asarray(a.astype(np.float32).astype(BF16))
    return (as_bf16(f1), as_bf16(g1), jnp.asarray(tw.astype(np.float32)), as_bf16(f2), as_bf16(g2), as_bf16(order))


def kernel(
    plan, tokens, in_w, spec, out_w, f1_h, g1_h, tw_h, f2_h, g2_h, ord_h, conv_w, skip_w, out,
    w_all, tok_v, acc, spec_v, ord_v, spec_s, spec_r, spec_f, proj_s, proj_r, proj_f,
    gate_f, gate_s, gate_r, gate_a, ow, o_acc, o_own, o_far, f1, g1, tw, f2, g2,
    load_sem, ring_send, ring_recv, ring2_send, ring2_recv, x_send, x_recv, w_send, w_recv,
    a2a_send, a2a_recv, ow_send, ow_recv, out_send, out_recv,
):
    ns, nz, nch, n_y, half, ds, ec, cpd = plan.ns, plan.nz, plan.nch, plan.n_y, plan.half, plan.ds, plan.ec, plan.cpd
    s, c = lax.axis_index("seq"), lax.axis_index("chan")
    core, xh, y = lax.rem(s, 2), lax.rem(s // 2, plan.x_hi), s // (2 * plan.x_hi)
    xl, z = c // nz, lax.rem(c, nz)
    other = 1 - xl
    partner = other * nz + z
    me, here, peers = xl * ns + s, 2 * s + xl, 2 * ns
    hops = nz // 2
    part = half // 2
    wide = 3 * cpd

    def seq_of(y_, xh_, core_):
        return (y_ * plan.x_hi + xh_) * 2 + core_

    def remote(src, dst, ss, rs, seq, chan):
        return pltpu.make_async_remote_copy(
            src_ref=src, dst_ref=dst, send_sem=ss, recv_sem=rs,
            device_id={"seq": seq, "chan": chan}, device_id_type=MESH,
        )

    def arrived(ref, sem):
        pltpu.make_async_copy(ref, ref, sem).wait()

    def place(grp, off):
        k = min(off, nz - off) if isinstance(off, int) else jnp.minimum(off, nz - off)
        return 4 * k - 2 + 2 * ((nz - 1 - off) // hops) + grp

    def origin(side, at):
        grp, off = next((g, o) for g in range(2) for o in range(nz) if place(g, o) == at)
        return (side if grp == 0 else 1 - side) * nz + lax.rem(z + off, nz)

    def rows_of(block):
        return pl.ds(pl.multiple_of(block * ds, ds), ds)

    def start_weights():
        for at in range(nch):
            rows = rows_of(origin(xl, at))
            for p in range(3):
                pltpu.make_async_copy(
                    in_w.at[p, rows, :], w_all.at[at * ds : (at + 1) * ds, p * cpd : (p + 1) * cpd], load_sem.at[1]
                ).start()

    loads = [pltpu.make_async_copy(tokens.at[pl.ds(xl * half, half), :], tok_v.at[:, 0:ds], load_sem.at[0])]
    loads += [pltpu.make_async_copy(a, b, load_sem.at[2 + i]) for i, (a, b) in enumerate(
        [(ord_h, ord_v), (f1_h, f1), (g1_h, g1), (tw_h, tw), (f2_h, f2), (g2_h, g2)])]
    spec_loads = [
        pltpu.make_async_copy(spec.at[p, :, k, :], spec_v.at[p, k], load_sem.at[8 + 2 * p + k])
        for p in range(2) for k in range(2)
    ]

    bar = pltpu.get_barrier_semaphore()

    def greet_plane(d, carry):
        q = lax.rem(me + d, peers)
        pl.semaphore_signal(bar, inc=1, device_id={"seq": lax.rem(q, ns), "chan": (q // ns) * nz + z}, device_id_type=MESH)
        return carry

    def greet_line(d, carry):
        pl.semaphore_signal(bar, inc=1, device_id={"seq": s, "chan": xl * nz + lax.rem(z + d, nz)}, device_id_type=MESH)
        return carry

    lax.fori_loop(1, peers, greet_plane, 0)
    lax.fori_loop(1, nz, greet_line, 0)
    for cp in loads[:2] + spec_loads:
        cp.start()
    start_weights()
    for cp in loads[2:]:
        cp.start()
    pl.semaphore_wait(bar, peers - 1 + nz - 1)

    reach = {(0, 0): hops, (1, 0): nz - 1 - hops, (0, 1): nz - 1 - hops, (1, 1): hops}
    sent = []

    def go(cp):
        cp.start()
        sent.append(cp)

    class Ring:
        def __init__(self, buf, width, send, recv):
            self.buf, self.width, self.send, self.recv = buf, width, send, recv

        def item(self, r, way, grp, k):
            at = place(grp, (nz - k if way == 0 else k) % nz)
            return self.buf.at[r * part : (r + 1) * part, at * self.width : (at + 1) * self.width]

        def hand_on(self, r, way, grp, k, src=None):
            to = lax.rem(z + 1, nz) if way == 0 else lax.rem(z + nz - 1, nz)
            go(remote(
                self.item(r, way, grp, k) if src is None else src, self.item(r, way, grp, k + 1),
                self.send.at[r, way, grp, k], self.recv.at[r, way, grp, k], s, xl * nz + to,
            ))

        def begin(self, r, grp, src=None):
            for way in range(2):
                if reach[way, grp] > 0:
                    self.hand_on(r, way, grp, 0, src)

        def step(self, r, k):
            for grp in range(2):
                for way in range(2):
                    if k <= reach[way, grp]:
                        arrived(self.item(r, way, grp, k), self.recv.at[r, way, grp, k - 1])
                        if k < reach[way, grp]:
                            self.hand_on(r, way, grp, k)

    def token_rows(side, r):
        return tokens.at[pl.ds(pl.multiple_of(side * half + r * part, part), part), :]

    ring = Ring(tok_v, ds, ring_send, ring_recv)
    far_home = tok_v.at[:, ds : 2 * ds]

    def swap(r):
        go(remote(token_rows(other, r), far_home.at[r * part : (r + 1) * part, :], x_send.at[r], x_recv.at[r], s, partner))

    swap(0)
    ring.begin(0, 0, token_rows(xl, 0))
    swap(1)

    quarter = nch // 4

    def far_rows(i):
        q = (2 * core + i) * quarter * ds
        return pl.ds(pl.multiple_of(q, quarter * ds), quarter * ds)

    for i, xh_ in ((0, lax.rem(xh + xl, plan.x_hi)), (1, lax.rem(xh + plan.x_hi - 1 + xl, plan.x_hi))):
        for j in range(quarter):
            first, second = origin(other, i * quarter + j), origin(other, (2 + i) * quarter + j)
            rows = rows_of(first + core * (second - first))
            to = pl.ds(pl.multiple_of((2 * core + i) * quarter * ds + j * ds, ds), ds)
            for p in range(3):
                remote(
                    in_w.at[p, rows, :], w_all.at[to, wide + p * cpd : wide + (p + 1) * cpd],
                    w_send.at[i], w_recv.at[i], seq_of(y, xh_, core), partner,
                ).start()

    row = pl.ds(pl.multiple_of((core * n_y + y) * plan.piece, plan.piece), plan.piece)
    if plan.x_hi == 2:
        sides = [(xh, pl.ds(pl.multiple_of(xh * ec, ec), ec))]
    else:
        sides = [(0, pl.ds(0, ec)), (1, pl.ds(ec, ec))]

    def out_cols(g, zz):
        return pl.ds(pl.multiple_of((g * nz + zz) * ec, ec), ec)

    def ow_first(d, carry):
        zz = lax.rem(z + d, nz)
        at = place(0, nz - d) // 2
        for g, to in sides:
            remote(out_w.at[row, out_cols(g, zz)], ow.at[at, 0, row, to], ow_send.at[0], ow_recv.at[0], s, xl * nz + zz).start()
        return carry

    lax.fori_loop(1, nz, ow_first, 0)
    ow_own = [
        pltpu.make_async_copy(out_w.at[row, out_cols(g, z)], ow.at[0, 0, row, to], load_sem.at[12 + i])
        for i, (g, to) in enumerate(sides)
    ]
    for cp in ow_own:
        cp.start()

    arrived(far_home.at[0:part, :], x_recv.at[0])
    ring.begin(0, 1)

    loads[1].wait()
    for p in range(2):
        turned = []
        for k in range(2):
            spec_loads[2 * p + k].wait()
            turned.append(jnp.dot(spec_v[p, k].astype(BF16), ord_v[...], preferred_element_type=F32))
        for m in range(plan.m):
            pair = [t[:, m * LANES : (m + 1) * LANES].reshape(ns, SUB, LANES) for t in turned]
            spec_s[:, p, m] = jnp.concatenate(pair, axis=1).astype(BF16)
    spec_own = pltpu.make_async_copy(spec_s.at[s], spec_r.at[s], load_sem.at[14])
    spec_own.start()

    def send_spec(d, carry):
        q = lax.rem(s + d, ns)
        remote(spec_s.at[q], spec_r.at[s], a2a_send.at[0], a2a_recv.at[0], q, c).start()
        return carry

    def pack(value, r, g, p):
        pair = [value[i * LANES : (i + 1) * LANES, :].T.reshape(ns, SUB, LANES) for i in range(2)]
        at = xl if g == 0 else other
        proj_s[pl.ds(at * ns, ns), r, p] = jnp.concatenate(pair, axis=1).astype(BF16)

    def send_proj(r, g):
        def one(d, carry):
            q = lax.rem(s + d, ns)
            remote(
                proj_s.at[(xl if g == 0 else other) * ns + q, r], proj_r.at[here, r], a2a_send.at[1 + r], a2a_recv.at[1 + r],
                q, c if g == 0 else partner,
            ).start()
            return carry

        lax.fori_loop(1 - g, ns, one, 0)
        if g == 0:
            pltpu.make_async_copy(proj_s.at[me, r], proj_r.at[here, r], load_sem.at[15 + r]).start()

    def project(r, g):
        rows = slice(r * part, (r + 1) * part)
        value = jnp.dot(tok_v[rows, :], w_all[:, g * wide : (g + 1) * wide], preferred_element_type=F32)
        for p in range(3):
            pack(value[:, p * cpd : (p + 1) * cpd], r, g, p)
        send_proj(r, g)

    def ow_second():
        for cp in ow_own:
            cp.wait()
        mine = ow.at[:, 0, row, sides[0][1]] if plan.x_hi == 2 else ow.at[:, 0, row, :]
        arrived(mine.at[0 : nz - 1], ow_recv.at[0])
        far = ow.at[:, 1, row, sides[0][1]] if plan.x_hi == 2 else ow.at[:, 1, row, :]
        go(remote(mine, far, ow_send.at[1], ow_recv.at[1], s, partner))
        if plan.x_hi == 2:
            go(remote(mine, mine, ow_send.at[2], ow_recv.at[2], seq_of(y, 1 - xh, core), c))
            go(remote(mine, far, ow_send.at[3], ow_recv.at[3], seq_of(y, 1 - xh, core), partner))

    def ow_third():
        if plan.x_hi == 2:
            away = pl.ds(pl.multiple_of((1 - xh) * ec, ec), ec)
            arrived(ow.at[:, 1, row, sides[0][1]], ow_recv.at[1])
            arrived(ow.at[:, 0, row, away], ow_recv.at[2])
            arrived(ow.at[:, 1, row, away], ow_recv.at[3])
        else:
            arrived(ow.at[:, 1, row, :], ow_recv.at[1])
        for dy in range(1, n_y):
            go(remote(ow.at[:, :, row, :], ow.at[:, :, row, :], ow_send.at[3 + dy], ow_recv.at[3 + dy],
                      seq_of(lax.rem(y + dy, n_y), xh, core), c))

    half_ow = n_y * plan.piece

    def ow_fourth():
        for dy in range(1, n_y):
            yy = lax.rem(y + n_y - dy, n_y)
            piece = pl.ds(pl.multiple_of((core * n_y + yy) * plan.piece, plan.piece), plan.piece)
            arrived(ow.at[:, :, piece, :], ow_recv.at[3 + dy])
        side = pl.ds(pl.multiple_of(core * half_ow, half_ow), half_ow)
        go(remote(ow.at[:, :, side, :], ow.at[:, :, side, :], ow_send.at[3 + n_y], ow_recv.at[3 + n_y], seq_of(y, xh, 1 - core), c))

    def ow_last():
        away = pl.ds(pl.multiple_of((1 - core) * half_ow, half_ow), half_ow)
        arrived(ow.at[:, :, away, :], ow_recv.at[3 + n_y])

    def far_pass():
        for i in range(2):
            arrived(w_all.at[far_rows(i), wide : 2 * wide], w_recv.at[i])
        side = pl.ds(pl.multiple_of(core * 2 * quarter * ds, 2 * quarter * ds), 2 * quarter * ds)
        mine = w_all.at[side, wide : 2 * wide]
        go(remote(mine, mine, w_send.at[2], w_recv.at[2], seq_of(y, xh, 1 - core), c))

    def far_wait():
        away = pl.ds(pl.multiple_of((1 - core) * 2 * quarter * ds, 2 * quarter * ds), 2 * quarter * ds)
        arrived(w_all.at[away, wide : 2 * wide], w_recv.at[2])

    for k in range(1, hops + 1):
        ring.step(0, k)
        if k == max(hops - 1, 1):
            arrived(far_home.at[part : 2 * part, :], x_recv.at[1])
            ring.begin(1, 0, token_rows(xl, 1))
            ring.begin(1, 1)
        if k == 1:
            ow_second()
    loads[0].wait()
    arrived(w_all.at[:, 0:wide], load_sem.at[1])
    ow_third()
    project(0, 0)
    for k in range(1, hops):
        ring.step(1, k)
        if k == 1:
            far_pass()
            lax.fori_loop(1, ns, send_spec, 0)
        if k == 2:
            far_wait()
            project(0, 1)
    if hops < 2:
        far_pass()
        lax.fori_loop(1, ns, send_spec, 0)
    if hops < 3:
        far_wait()
        project(0, 1)
    ow_fourth()
    bulk = (nch - 2) * ds
    rows = slice(part, 2 * part)
    for g in range(2):
        for p in range(3):
            at = g * wide + p * cpd
            if (at // cpd) % 2 == 0:
                acc[:, at : at + 2 * cpd] = jnp.dot(
                    tok_v[rows, 0:bulk], w_all[0:bulk, at : at + 2 * cpd], preferred_element_type=F32)
    ring.step(1, hops)
    rest = acc[...] + jnp.dot(tok_v[rows, bulk:], w_all[bulk:, :], preferred_element_type=F32)
    for g in range(2):
        for p in range(3):
            at = g * wide + p * cpd
            pack(rest[:, at : at + cpd], 1, g, p)
        send_proj(1, g)

    spec_own.wait()
    arrived(spec_r.at[0 : ns - 1], a2a_recv.at[0])

    def lay(i, carry):
        for p in range(2):
            for m in range(plan.m):
                spec_f[p, pl.ds(pl.multiple_of((m * ns + i) * 16, 16), 16), :] = spec_r[i, p, m].astype(F32)
        return carry

    lax.fori_loop(0, ns, lay, 0)
    for cp in loads[2:]:
        cp.wait()
    for r in range(2):
        arrived(proj_r.at[here, r], load_sem.at[15 + r])
        arrived(proj_r.at[0 : peers - 1, r], a2a_recv.at[1 + r])
    for p in range(3):
        proj_f[p] = proj_r[:, :, p].astype(F32).reshape(plan.nhi * SUB, LANES)

    lane = lax.broadcasted_iota(jnp.int32, (plan.nhi, LANES), 1)
    posn = lane + LANES * lax.broadcasted_iota(jnp.int32, (plan.nhi, LANES), 0)

    def behind(x, by):
        turned = pltpu.roll(x, by, 1)
        both = jnp.where(lane < by, pltpu.roll(turned, 1, 0), turned)
        return jnp.where(posn < by, 0.0, both)

    def transform(ch, carry):
        chan = s * SUB + ch
        parts = []
        for p in range(3):
            x = proj_f[p, pl.ds(ch, plan.nhi, stride=SUB), :]
            f = conv_w[0, p, chan] * x
            for j in range(1, 3):
                f = f + conv_w[j, p, chan] * behind(x, j)
            parts.append(f)
        query, signal = parts[0], (parts[1] * parts[2]).astype(BF16)
        a = jnp.dot(f1[...], signal, preferred_element_type=F32)
        ar, ai = a[: plan.ka], a[plan.ka :]
        tr, ti = tw[0], tw[1]
        yy = jnp.concatenate([(ar * tr - ai * ti).astype(BF16), (ar * ti + ai * tr).astype(BF16)], axis=1)
        zz = jnp.dot(yy, f2[...], preferred_element_type=F32)
        zr, zi = zz[:, :LANES], zz[:, LANES:]
        hr, hi = (spec_f[p, pl.ds(ch, plan.ka, stride=SUB), :] for p in range(2))
        pp = jnp.concatenate([(zr * hr - zi * hi).astype(BF16), (zr * hi + zi * hr).astype(BF16)], axis=1)
        u = jnp.dot(pp, g2[...], preferred_element_type=F32)
        ur, ui = u[:, :LANES], u[:, LANES:]
        v = jnp.concatenate([(ur * tr + ui * ti).astype(BF16), (ui * tr - ur * ti).astype(BF16)], axis=0)
        longconv = jnp.dot(g1[...], v, preferred_element_type=F32)
        gate_f[pl.ds(ch, plan.nhi, stride=SUB), :] = query * (longconv + skip_w[chan] * signal.astype(F32))
        return carry

    lax.fori_loop(0, SUB, transform, 0, unroll=True)
    gate_s[...] = gate_f[...].astype(BF16).reshape(peers, plan.rows, LANES)

    def send_gate(d, carry):
        q = lax.rem(here + d, peers)
        remote(gate_s.at[q], gate_r.at[me], a2a_send.at[3], a2a_recv.at[3], q // 2, lax.rem(q, 2) * nz + z).start()
        return carry

    lax.fori_loop(1, peers, send_gate, 0)
    gate_own = pltpu.make_async_copy(gate_s.at[here], gate_r.at[me], load_sem.at[17])
    gate_own.start()
    gate_own.wait()
    arrived(gate_r.at[0 : peers - 1], a2a_recv.at[3])

    ring2 = Ring(gate_a, cpd, ring2_send, ring2_recv)

    def repack(r):
        for grp in range(2):
            pair = gate_r[pl.ds((xl if grp == 0 else other) * ns, ns), 16 * r : 16 * (r + 1), :].astype(F32)
            for i in range(2):
                block = pair[:, SUB * i : SUB * (i + 1), :].reshape(cpd, LANES)
                at = r * part + i * LANES
                gate_a[at : at + LANES, grp * cpd : (grp + 1) * cpd] = block.T.astype(BF16)
            ring2.begin(r, grp)

    k_bulk = (nch - 2) * cpd

    def weights(lo, hi):
        return ow[lo // (2 * cpd) : hi // (2 * cpd)].reshape(hi - lo, 2 * ec)

    def mix(r):
        rows = slice(r * part, (r + 1) * part)
        o_acc[...] = jnp.dot(gate_a[rows, 0:k_bulk], weights(0, k_bulk), preferred_element_type=F32)

    def finish(r):
        rows = slice(r * part, (r + 1) * part)
        total = o_acc[...] + jnp.dot(gate_a[rows, k_bulk:], weights(k_bulk, nch * cpd), preferred_element_type=F32)
        left, right = total[:, :ec].astype(BF16), total[:, ec:].astype(BF16)
        o_far[r] = jnp.where(xl == 0, right, left)
        mine = out.at[pl.ds(pl.multiple_of(xl * half + r * part, part), part), :]
        go(remote(o_far.at[r], mine, out_send.at[r], out_recv.at[r], s, partner))
        o_own[r] = jnp.where(xl == 0, left, right)
        pltpu.make_async_copy(o_own.at[r], mine, load_sem.at[18 + r]).start()

    repack(0)
    ow_last()
    order = []
    for t in range(1, hops + 2):
        if t <= hops:
            order.append((0, t))
        order.append((1, t - 1))
    for r, k in order:
        if k == 0:
            repack(r)
            continue
        if k == hops:
            mix(r)
        ring2.step(r, k)
        if k == hops:
            finish(r)

    for cp in sent:
        cp.wait_send()
    for i in range(2):
        arrived(w_all.at[0 : quarter * ds, wide : 2 * wide], w_send.at[i])
        arrived(proj_s.at[0 : peers - 1, i], a2a_send.at[1 + i])
        mine = out.at[pl.ds(pl.multiple_of(xl * half + i * part, part), part), :]
        theirs = out.at[pl.ds(pl.multiple_of(other * half + i * part, part), part), :]
        arrived(mine, load_sem.at[18 + i])
        arrived(theirs, out_recv.at[i])
    arrived(spec_s.at[0 : ns - 1], a2a_send.at[0])
    arrived(gate_s.at[0 : peers - 1], a2a_send.at[3])
    legs = ow.at[0 : nz - 1, 0, row, sides[0][1]] if plan.x_hi == 2 else ow.at[0 : nz - 1, 0, row, :]
    arrived(legs, ow_send.at[0])


def make(plan):
    consts = tables(plan)

    def shards(tokens, in_weight, conv_weight, spectrum, skip, out_weight):
        ns, peers, cpd = plan.ns, 2 * plan.ns, plan.cpd
        hops = plan.nz // 2
        vm = pltpu.VMEM
        dma = pltpu.SemaphoreType.DMA
        anywhere = pl.BlockSpec(memory_space=pl.ANY)
        scalars = pl.BlockSpec(memory_space=pltpu.SMEM)
        return pl.pallas_call(
            lambda *refs: kernel(plan, *refs),
            out_shape=jax.ShapeDtypeStruct((plan.tok, plan.ec), BF16),
            in_specs=[anywhere] * 10 + [scalars] * 2,
            out_specs=anywhere,
            scratch_shapes=[
                vm((plan.d, 6 * cpd), BF16),
                vm((plan.half, plan.d), BF16),
                vm((plan.half // 2, 6 * cpd), F32),
                vm((2, 2, cpd, plan.k2), F32), vm((plan.k2, plan.k2), BF16),
                vm((ns, 2, plan.m, 16, LANES), BF16), vm((ns, 2, plan.m, 16, LANES), BF16),
                vm((2, plan.m * ns * 16, LANES), F32),
                vm((peers, 2, 3, 16, LANES), BF16), vm((peers, 2, 3, 16, LANES), BF16),
                vm((3, plan.nhi * SUB, LANES), F32),
                vm((plan.nhi * SUB, LANES), F32),
                vm((peers, plan.rows, LANES), BF16), vm((peers, plan.rows, LANES), BF16),
                vm((plan.half, plan.nch * cpd), BF16),
                vm((plan.nz, 2, cpd, 2 * plan.ec), BF16),
                vm((plan.half // 2, 2 * plan.ec), F32),
                vm((2, plan.half // 2, plan.ec), BF16), vm((2, plan.half // 2, plan.ec), BF16),
                vm((2 * plan.ka, plan.nhi), BF16), vm((plan.nhi, 2 * plan.ka), BF16),
                vm((2, plan.ka, LANES), F32),
                vm((2 * LANES, 2 * LANES), BF16), vm((2 * LANES, 2 * LANES), BF16),
                dma((20,)), dma((2, 2, 2, hops)), dma((2, 2, 2, hops)), dma((2, 2, 2, hops)), dma((2, 2, 2, hops)),
                dma((2,)), dma((2,)), dma((3,)), dma((3,)), dma((4,)), dma((4,)),
                dma((plan.n_y + 4,)), dma((plan.n_y + 4,)), dma((2,)), dma((2,)),
            ],
            compiler_params=pltpu.CompilerParams(
                collective_id=0, has_side_effects=True, vmem_limit_bytes=56 * 1024 * 1024
            ),
            name="hyena",
        )(tokens, in_weight, spectrum, out_weight, *consts, conv_weight, skip)

    return shards


def on_mesh(mesh, plan):
    placed = (
        P("seq", "chan"),
        P(None, None, "chan"),
        P(None, None, "chan"),
        P(None, "chan", "seq", None),
        P("chan"),
        P("chan", None),
    )
    return jax.shard_map(make(plan), mesh=mesh, in_specs=placed, out_specs=P("seq", "chan"), check_vma=False)


def solution(mesh):
    return on_mesh(mesh, Plan(ns=16, nch=16, n_y=4, x_hi=2, tok=1024, ds=256, ec=256))
```

```python
import math

import jax
import jax.numpy as jnp
import numpy as np
from jax import lax
from jax.experimental import pallas as pl
from jax.experimental.pallas import tpu as pltpu
from jax.sharding import PartitionSpec as P

MESH = pl.DeviceIdType.MESH
LANES = 128
SUB = 8
BF16 = jnp.bfloat16
F32 = jnp.float32


class Plan:
    def __init__(self, ns, nch, n_y, x_hi, tok, ds, ec):
        self.ns, self.nch, self.nz, self.n_y, self.x_hi = ns, nch, nch // 2, n_y, x_hi
        self.tok, self.half, self.ds, self.ec = tok, tok // 2, ds, ec
        self.cpd = SUB * ns
        self.d, self.e = nch * ds, nch * ec
        self.nhi = ns * tok // LANES
        self.ka = 2 * self.nhi
        self.nfft = 2 * ns * tok
        self.k1 = 2 * ns
        self.m = self.ka // self.k1
        self.k2 = self.m * LANES
        self.blocks = self.half // LANES
        self.rows = self.blocks * SUB
        self.piece = self.cpd // (2 * n_y)


def tables(plan):
    m, s, k1l = np.meshgrid(np.arange(plan.m), np.arange(plan.ns), np.arange(2), indexing="ij")
    ka = (2 * s + k1l + plan.k1 * m).reshape(-1).astype(np.int64)
    nhi = np.arange(plan.nhi, dtype=np.int64)
    lane = np.arange(LANES, dtype=np.int64)

    def angle(a, b, mod):
        return (a[:, None] * b[None, :] % mod) * (2.0 * math.pi / mod)

    left = angle(ka, nhi, plan.ka)
    f1 = np.concatenate([np.cos(left), -np.sin(left)], axis=0)
    g1 = np.concatenate([np.cos(left.T), -np.sin(left.T)], axis=1) / plan.nfft
    turn = angle(ka, lane, plan.nfft)
    tw = np.stack([np.cos(turn), -np.sin(turn)])
    right = angle(lane, lane, LANES)
    c, sn = np.cos(right), np.sin(right)
    f2 = np.block([[c, -sn], [sn, c]])
    g2 = np.block([[c, sn], [-sn, c]])
    order = np.zeros((plan.k2, plan.k2), np.float32)
    k2 = np.arange(plan.k2)
    order[k2, (k2 % plan.m) * LANES + k2 // plan.m] = 1.0
    as_bf16 = lambda a: jnp.asarray(a.astype(np.float32).astype(BF16))
    return (as_bf16(f1), as_bf16(g1), jnp.asarray(tw.astype(np.float32)), as_bf16(f2), as_bf16(g2), as_bf16(order))


def kernel(
    plan, tokens, in_w, spec, out_w, f1_h, g1_h, tw_h, f2_h, g2_h, ord_h, conv_w, skip_w, out,
    w_all, tok_v, acc, spec_v, ord_v, spec_s, spec_r, spec_f, proj_s, proj_r, proj_f,
    gate_f, gate_s, gate_r, gate_a, ow, o_acc, o_own, o_far, f1, g1, tw, f2, g2,
    load_sem, ring_send, ring_recv, ring2_send, ring2_recv, x_send, x_recv, w_send, w_recv,
    a2a_send, a2a_recv, ow_send, ow_recv, out_send, out_recv,
):
    ns, nz, nch, n_y, half, ds, ec, cpd = plan.ns, plan.nz, plan.nch, plan.n_y, plan.half, plan.ds, plan.ec, plan.cpd
    s, c = lax.axis_index("seq"), lax.axis_index("chan")
    core, xh, y = lax.rem(s, 2), lax.rem(s // 2, plan.x_hi), s // (2 * plan.x_hi)
    xl, z = c // nz, lax.rem(c, nz)
    other = 1 - xl
    partner = other * nz + z
    me, here, peers = xl * ns + s, 2 * s + xl, 2 * ns
    hops = nz // 2
    part = half // 2
    wide = 3 * cpd

    def seq_of(y_, xh_, core_):
        return (y_ * plan.x_hi + xh_) * 2 + core_

    def remote(src, dst, ss, rs, seq, chan):
        return pltpu.make_async_remote_copy(
            src_ref=src, dst_ref=dst, send_sem=ss, recv_sem=rs,
            device_id={"seq": seq, "chan": chan}, device_id_type=MESH,
        )

    def arrived(ref, sem):
        pltpu.make_async_copy(ref, ref, sem).wait()

    def place(grp, off):
        k = min(off, nz - off) if isinstance(off, int) else jnp.minimum(off, nz - off)
        return 4 * k - 2 + 2 * ((nz - 1 - off) // hops) + grp

    def origin(side, at):
        grp, off = next((g, o) for g in range(2) for o in range(nz) if place(g, o) == at)
        return (side if grp == 0 else 1 - side) * nz + lax.rem(z + off, nz)

    def rows_of(block):
        return pl.ds(pl.multiple_of(block * ds, ds), ds)

    def start_weights():
        for at in range(nch):
            rows = rows_of(origin(xl, at))
            for p in range(3):
                pltpu.make_async_copy(
                    in_w.at[p, rows, :], w_all.at[at * ds : (at + 1) * ds, p * cpd : (p + 1) * cpd], load_sem.at[1]
                ).start()

    loads = [pltpu.make_async_copy(tokens.at[pl.ds(xl * half, half), :], tok_v.at[:, 0:ds], load_sem.at[0])]
    loads += [pltpu.make_async_copy(a, b, load_sem.at[2 + i]) for i, (a, b) in enumerate(
        [(ord_h, ord_v), (f1_h, f1), (g1_h, g1), (tw_h, tw), (f2_h, f2), (g2_h, g2)])]
    spec_loads = [
        pltpu.make_async_copy(spec.at[p, :, k, :], spec_v.at[p, k], load_sem.at[8 + 2 * p + k])
        for p in range(2) for k in range(2)
    ]

    def hop(by, size):
        return min(by, size - by)

    others = [(dy, dh, dl, dk) for dy in range(n_y) for dh in range(plan.x_hi) for dl in range(2) for dk in range(2)]
    others = sorted(others[1:], key=lambda o: -hop(o[0], n_y) - (2 if o[1] and not o[2] else int(bool(o[1] or o[2]))))

    def peer(o):
        dy, dh, dl, dk = o
        seq = seq_of(lax.rem(y + dy, n_y), lax.rem(xh + dh, plan.x_hi), lax.rem(core + dk, 2))
        return seq, xl if dl == 0 else other

    bar = pltpu.get_barrier_semaphore()

    def greet_plane(d, carry):
        q = lax.rem(me + d, peers)
        pl.semaphore_signal(bar, inc=1, device_id={"seq": lax.rem(q, ns), "chan": (q // ns) * nz + z}, device_id_type=MESH)
        return carry

    def greet_line(d, carry):
        pl.semaphore_signal(bar, inc=1, device_id={"seq": s, "chan": xl * nz + lax.rem(z + d, nz)}, device_id_type=MESH)
        return carry

    lax.fori_loop(1, peers, greet_plane, 0)
    lax.fori_loop(1, nz, greet_line, 0)
    for cp in loads[:2] + spec_loads:
        cp.start()
    start_weights()
    for cp in loads[2:]:
        cp.start()
    pl.semaphore_wait(bar, peers - 1 + nz - 1)

    reach = {(0, 0): hops, (1, 0): nz - 1 - hops, (0, 1): nz - 1 - hops, (1, 1): hops}
    sent = []

    def go(cp):
        cp.start()
        sent.append(cp)

    class Ring:
        def __init__(self, buf, width, parts, send, recv):
            self.buf, self.width, self.parts, self.send, self.recv = buf, width, parts, send, recv

        def item(self, r, way, grp, k):
            at = place(grp, (nz - k if way == 0 else k) % nz)
            lo, hi = self.parts[r]
            return self.buf.at[lo:hi, at * self.width : (at + 1) * self.width]

        def hand_on(self, r, way, grp, k, src=None):
            to = lax.rem(z + 1, nz) if way == 0 else lax.rem(z + nz - 1, nz)
            go(remote(
                self.item(r, way, grp, k) if src is None else src, self.item(r, way, grp, k + 1),
                self.send.at[r, way, grp, k], self.recv.at[r, way, grp, k], s, xl * nz + to,
            ))

        def begin(self, r, grp, src=None):
            for way in range(2):
                if reach[way, grp] > 0:
                    self.hand_on(r, way, grp, 0, src)

        def step(self, r, k):
            for grp in range(2):
                for way in range(2):
                    if k <= reach[way, grp]:
                        arrived(self.item(r, way, grp, k), self.recv.at[r, way, grp, k - 1])
                        if k < reach[way, grp]:
                            self.hand_on(r, way, grp, k)

    def token_rows(side, r):
        return tokens.at[pl.ds(pl.multiple_of(side * half + r * part, part), part), :]

    ring = Ring(tok_v, ds, [(0, part), (part, half)], ring_send, ring_recv)
    far_home = tok_v.at[:, ds : 2 * ds]

    def swap(r):
        go(remote(token_rows(other, r), far_home.at[r * part : (r + 1) * part, :], x_send.at[r], x_recv.at[r], s, partner))

    swap(0)
    ring.begin(0, 0, token_rows(xl, 0))
    swap(1)
    ring.begin(1, 0, token_rows(xl, 1))

    quarter = nch // 4

    def far_rows(i):
        q = (2 * core + i) * quarter * ds
        return pl.ds(pl.multiple_of(q, quarter * ds), quarter * ds)

    for i, xh_ in ((0, lax.rem(xh + xl, plan.x_hi)), (1, lax.rem(xh + plan.x_hi - 1 + xl, plan.x_hi))):
        for j in range(quarter):
            first, second = origin(other, i * quarter + j), origin(other, (2 + i) * quarter + j)
            rows = rows_of(first + core * (second - first))
            to = pl.ds(pl.multiple_of((2 * core + i) * quarter * ds + j * ds, ds), ds)
            for p in range(3):
                remote(
                    in_w.at[p, rows, :], w_all.at[to, wide + p * cpd : wide + (p + 1) * cpd],
                    w_send.at[i], w_recv.at[i], seq_of(y, xh_, core), partner,
                ).start()

    row = pl.ds(pl.multiple_of((core * n_y + y) * plan.piece, plan.piece), plan.piece)
    if plan.x_hi == 2:
        sides = [(xh, pl.ds(pl.multiple_of(xh * ec, ec), ec))]
    else:
        sides = [(0, pl.ds(0, ec)), (1, pl.ds(ec, ec))]

    def out_cols(g, zz):
        return pl.ds(pl.multiple_of((g * nz + zz) * ec, ec), ec)

    def ow_first(d, carry):
        zz = lax.rem(z + d, nz)
        at = place(0, nz - d) // 2
        for g, to in sides:
            remote(out_w.at[row, out_cols(g, zz)], ow.at[at, 0, row, to], ow_send.at[0], ow_recv.at[0], s, xl * nz + zz).start()
        return carry

    lax.fori_loop(1, nz, ow_first, 0)
    ow_own = [
        pltpu.make_async_copy(out_w.at[row, out_cols(g, z)], ow.at[0, 0, row, to], load_sem.at[12 + i])
        for i, (g, to) in enumerate(sides)
    ]
    for cp in ow_own:
        cp.start()

    arrived(far_home.at[0:part, :], x_recv.at[0])
    ring.begin(0, 1)

    loads[1].wait()
    for p in range(2):
        turned = []
        for k in range(2):
            spec_loads[2 * p + k].wait()
            turned.append(jnp.dot(spec_v[p, k].astype(BF16), ord_v[...], preferred_element_type=F32))
        for m in range(plan.m):
            pair = [t[:, m * LANES : (m + 1) * LANES].reshape(ns, SUB, LANES) for t in turned]
            spec_s[:, p, m] = jnp.concatenate(pair, axis=1).astype(BF16)
    spec_own = pltpu.make_async_copy(spec_s.at[s], spec_r.at[s], load_sem.at[14])
    spec_own.start()

    def send_spec(d, carry):
        q = lax.rem(s + d, ns)
        remote(spec_s.at[q], spec_r.at[s], a2a_send.at[0], a2a_recv.at[0], q, c).start()
        return carry

    lax.fori_loop(1, ns, send_spec, 0)

    def pack(value, r, g, p):
        pair = [value[i * LANES : (i + 1) * LANES, :].T.reshape(ns, SUB, LANES) for i in range(2)]
        at = xl if g == 0 else other
        proj_s[pl.ds(at * ns, ns), r, p] = jnp.concatenate(pair, axis=1).astype(BF16)

    def send_proj(r, g):
        for o in others:
            seq, side = peer(o)
            if o[2] == g:
                remote(
                    proj_s.at[side * ns + seq, r], proj_r.at[here, r], a2a_send.at[1 + r], a2a_recv.at[1 + r],
                    seq, side * nz + z,
                ).start()
        if g == 0:
            pltpu.make_async_copy(proj_s.at[me, r], proj_r.at[here, r], load_sem.at[15 + r]).start()

    def project(r, g):
        rows = slice(r * part, (r + 1) * part)
        value = jnp.dot(tok_v[rows, :], w_all[:, g * wide : (g + 1) * wide], preferred_element_type=F32)
        for p in range(3):
            pack(value[:, p * cpd : (p + 1) * cpd], r, g, p)
        send_proj(r, g)

    def ow_second():
        for cp in ow_own:
            cp.wait()
        mine = ow.at[:, 0, row, sides[0][1]] if plan.x_hi == 2 else ow.at[:, 0, row, :]
        arrived(mine.at[0 : nz - 1], ow_recv.at[0])
        far = ow.at[:, 1, row, sides[0][1]] if plan.x_hi == 2 else ow.at[:, 1, row, :]
        go(remote(mine, far, ow_send.at[1], ow_recv.at[1], s, partner))
        if plan.x_hi == 2:
            go(remote(mine, mine, ow_send.at[2], ow_recv.at[2], seq_of(y, 1 - xh, core), c))
            go(remote(mine, far, ow_send.at[3], ow_recv.at[3], seq_of(y, 1 - xh, core), partner))

    def ow_third():
        if plan.x_hi == 2:
            away = pl.ds(pl.multiple_of((1 - xh) * ec, ec), ec)
            arrived(ow.at[:, 1, row, sides[0][1]], ow_recv.at[1])
            arrived(ow.at[:, 0, row, away], ow_recv.at[2])
            arrived(ow.at[:, 1, row, away], ow_recv.at[3])
        else:
            arrived(ow.at[:, 1, row, :], ow_recv.at[1])
        for dy in range(1, n_y):
            go(remote(ow.at[:, :, row, :], ow.at[:, :, row, :], ow_send.at[3 + dy], ow_recv.at[3 + dy],
                      seq_of(lax.rem(y + dy, n_y), xh, core), c))

    half_ow = n_y * plan.piece

    def ow_fourth():
        for dy in range(1, n_y):
            yy = lax.rem(y + n_y - dy, n_y)
            piece = pl.ds(pl.multiple_of((core * n_y + yy) * plan.piece, plan.piece), plan.piece)
            arrived(ow.at[:, :, piece, :], ow_recv.at[3 + dy])
        side = pl.ds(pl.multiple_of(core * half_ow, half_ow), half_ow)
        go(remote(ow.at[:, :, side, :], ow.at[:, :, side, :], ow_send.at[3 + n_y], ow_recv.at[3 + n_y], seq_of(y, xh, 1 - core), c))

    def ow_last():
        away = pl.ds(pl.multiple_of((1 - core) * half_ow, half_ow), half_ow)
        arrived(ow.at[:, :, away, :], ow_recv.at[3 + n_y])

    def far_pass():
        for i in range(2):
            arrived(w_all.at[far_rows(i), wide : 2 * wide], w_recv.at[i])
        side = pl.ds(pl.multiple_of(core * 2 * quarter * ds, 2 * quarter * ds), 2 * quarter * ds)
        mine = w_all.at[side, wide : 2 * wide]
        go(remote(mine, mine, w_send.at[2], w_recv.at[2], seq_of(y, xh, 1 - core), c))

    def far_wait():
        away = pl.ds(pl.multiple_of((1 - core) * 2 * quarter * ds, 2 * quarter * ds), 2 * quarter * ds)
        arrived(w_all.at[away, wide : 2 * wide], w_recv.at[2])

    def own_wait():
        loads[0].wait()
        arrived(w_all.at[:, 0:wide], load_sem.at[1])

    def begin_second():
        arrived(far_home.at[part : 2 * part, :], x_recv.at[1])
        ring.begin(1, 1)

    bulk = (nch - 2) * ds
    rows = slice(part, 2 * part)

    def bulk_second():
        for at in range(0, 2 * wide, 2 * cpd):
            acc[:, at : at + 2 * cpd] = jnp.dot(
                tok_v[rows, 0:bulk], w_all[0:bulk, at : at + 2 * cpd], preferred_element_type=F32)

    after = {}
    steps = sorted((k + r * (hops - 1), r, k) for r in range(2) for k in range(1, hops + 1))
    place_of = {(r, k): i for i, (_, r, k) in enumerate(steps)}

    def hook(r, k, *does):
        k = max(1, min(k, hops))
        after.setdefault(place_of[r, k], []).extend(does)

    hook(0, hops - 1, begin_second, ow_second)
    hook(0, hops, own_wait, lambda: project(0, 0))
    hook(1, min(1, hops - 1), far_pass)
    hook(1, min(2, hops - 1), far_wait, lambda: project(0, 1))
    hook(1, hops - 1, bulk_second)
    for i, (_, r, k) in enumerate(steps):
        ring.step(r, k)
        for do in after.get(i, []):
            do()
    rest = acc[...] + jnp.dot(tok_v[rows, bulk:], w_all[bulk:, :], preferred_element_type=F32)
    for g in range(2):
        for p in range(3):
            at = g * wide + p * cpd
            pack(rest[:, at : at + cpd], 1, g, p)
        send_proj(1, g)

    spec_own.wait()
    arrived(spec_r.at[0 : ns - 1], a2a_recv.at[0])

    def lay(i, carry):
        for p in range(2):
            for m in range(plan.m):
                spec_f[p, pl.ds(pl.multiple_of((m * ns + i) * 16, 16), 16), :] = spec_r[i, p, m].astype(F32)
        return carry

    lax.fori_loop(0, ns, lay, 0)
    for cp in loads[2:]:
        cp.wait()
    for r in range(2):
        arrived(proj_r.at[here, r], load_sem.at[15 + r])
        arrived(proj_r.at[0 : peers - 1, r], a2a_recv.at[1 + r])
        for p in range(3):
            for q in range(peers):
                proj_f[p, q * plan.rows + 16 * r : q * plan.rows + 16 * (r + 1), :] = proj_r[q, r, p].astype(F32)

    lane = lax.broadcasted_iota(jnp.int32, (plan.nhi, LANES), 1)
    posn = lane + LANES * lax.broadcasted_iota(jnp.int32, (plan.nhi, LANES), 0)

    def behind(x, by):
        turned = pltpu.roll(x, by, 1)
        both = jnp.where(lane < by, pltpu.roll(turned, 1, 0), turned)
        return jnp.where(posn < by, 0.0, both)

    def transform(ch, carry):
        chan = s * SUB + ch
        parts = []
        for p in range(3):
            x = proj_f[p, pl.ds(ch, plan.nhi, stride=SUB), :]
            f = conv_w[0, p, chan] * x
            for j in range(1, 3):
                f = f + conv_w[j, p, chan] * behind(x, j)
            parts.append(f)
        query, signal = parts[0], (parts[1] * parts[2]).astype(BF16)
        a = jnp.dot(f1[...], signal, preferred_element_type=F32)
        ar, ai = a[: plan.ka], a[plan.ka :]
        tr, ti = tw[0], tw[1]
        yy = jnp.concatenate([(ar * tr - ai * ti).astype(BF16), (ar * ti + ai * tr).astype(BF16)], axis=1)
        zz = jnp.dot(yy, f2[...], preferred_element_type=F32)
        zr, zi = zz[:, :LANES], zz[:, LANES:]
        hr, hi = (spec_f[p, pl.ds(ch, plan.ka, stride=SUB), :] for p in range(2))
        pp = jnp.concatenate([(zr * hr - zi * hi).astype(BF16), (zr * hi + zi * hr).astype(BF16)], axis=1)
        u = jnp.dot(pp, g2[...], preferred_element_type=F32)
        ur, ui = u[:, :LANES], u[:, LANES:]
        v = jnp.concatenate([(ur * tr + ui * ti).astype(BF16), (ui * tr - ur * ti).astype(BF16)], axis=0)
        longconv = jnp.dot(g1[...], v, preferred_element_type=F32)
        gate_f[pl.ds(ch, plan.nhi, stride=SUB), :] = query * (longconv + skip_w[chan] * signal.astype(F32))
        return carry

    lax.fori_loop(0, SUB, transform, 0, unroll=True)
    gate_s[...] = gate_f[...].astype(BF16).reshape(peers, plan.rows, LANES)

    for o in others:
        seq, side = peer(o)
        remote(gate_s.at[2 * seq + side], gate_r.at[me], a2a_send.at[3], a2a_recv.at[3], seq, side * nz + z).start()
    gate_own = pltpu.make_async_copy(gate_s.at[here], gate_r.at[me], load_sem.at[17])
    gate_own.start()
    gate_own.wait()
    arrived(gate_r.at[0 : peers - 1], a2a_recv.at[3])

    parts2 = [(0, part), (part, half)]
    ring2 = Ring(gate_a, cpd, parts2, ring2_send, ring2_recv)

    def repack(r):
        lo, hi = parts2[r]
        for grp in range(2):
            for j in range(lo // LANES, hi // LANES):
                rows = gate_r[pl.ds((xl if grp == 0 else other) * ns, ns), 16 * (j // 2) : 16 * (j // 2 + 1), :].astype(F32)
                block = rows[:, SUB * (j % 2) : SUB * (j % 2 + 1), :].reshape(cpd, LANES)
                gate_a[j * LANES : (j + 1) * LANES, grp * cpd : (grp + 1) * cpd] = block.T.astype(BF16)
            ring2.begin(r, grp)

    k_bulk = (nch - 2) * cpd

    def weights(lo, hi):
        return ow[lo // (2 * cpd) : hi // (2 * cpd)].reshape(hi - lo, 2 * ec)

    def mix(r):
        lo, hi = parts2[r]
        o_acc[lo:hi, :] = jnp.dot(gate_a[lo:hi, 0:k_bulk], weights(0, k_bulk), preferred_element_type=F32)

    def own_rows(side, r):
        lo, hi = parts2[r]
        return out.at[pl.ds(pl.multiple_of(side * half + lo, LANES), hi - lo), :]

    def finish(r):
        lo, hi = parts2[r]
        total = o_acc[lo:hi, :] + jnp.dot(gate_a[lo:hi, k_bulk:], weights(k_bulk, nch * cpd), preferred_element_type=F32)
        left, right = total[:, :ec].astype(BF16), total[:, ec:].astype(BF16)
        o_far[lo:hi, :] = jnp.where(xl == 0, right, left)
        go(remote(o_far.at[lo:hi, :], own_rows(xl, r), out_send.at[r], out_recv.at[r], s, partner))
        o_own[lo:hi, :] = jnp.where(xl == 0, left, right)
        pltpu.make_async_copy(o_own.at[lo:hi, :], own_rows(xl, r), load_sem.at[18 + r]).start()

    ow_third()
    repack(0)
    order = sorted((k, r, k) for r in range(2) for k in range(hops + 1) if r + k > 0)
    for _, r, k in order:
        if k == 0:
            repack(r)
            continue
        if (r, k) == (1, max(hops - 1, 1)):
            ow_fourth()
        if k == hops:
            if r == 0:
                ow_last()
            mix(r)
        ring2.step(r, k)
        if k == hops:
            finish(r)

    for cp in sent:
        cp.wait_send()
    for i in range(2):
        arrived(w_all.at[0 : quarter * ds, wide : 2 * wide], w_send.at[i])
        arrived(proj_s.at[0 : peers - 1, i], a2a_send.at[1 + i])
    arrived(spec_s.at[0 : ns - 1], a2a_send.at[0])
    arrived(gate_s.at[0 : peers - 1], a2a_send.at[3])
    legs = ow.at[0 : nz - 1, 0, row, sides[0][1]] if plan.x_hi == 2 else ow.at[0 : nz - 1, 0, row, :]
    arrived(legs, ow_send.at[0])
    for r in range(2):
        arrived(own_rows(xl, r), load_sem.at[18 + r])
        arrived(own_rows(other, r), out_recv.at[r])


def make(plan):
    consts = tables(plan)

    def shards(tokens, in_weight, conv_weight, spectrum, skip, out_weight):
        ns, peers, cpd = plan.ns, 2 * plan.ns, plan.cpd
        hops = plan.nz // 2
        vm = pltpu.VMEM
        dma = pltpu.SemaphoreType.DMA
        anywhere = pl.BlockSpec(memory_space=pl.ANY)
        scalars = pl.BlockSpec(memory_space=pltpu.SMEM)
        return pl.pallas_call(
            lambda *refs: kernel(plan, *refs),
            out_shape=jax.ShapeDtypeStruct((plan.tok, plan.ec), BF16),
            in_specs=[anywhere] * 10 + [scalars] * 2,
            out_specs=anywhere,
            scratch_shapes=[
                vm((plan.d, 6 * cpd), BF16),
                vm((plan.half, plan.d), BF16),
                vm((plan.half // 2, 6 * cpd), F32),
                vm((2, 2, cpd, plan.k2), F32), vm((plan.k2, plan.k2), BF16),
                vm((ns, 2, plan.m, 16, LANES), BF16), vm((ns, 2, plan.m, 16, LANES), BF16),
                vm((2, plan.m * ns * 16, LANES), F32),
                vm((peers, 2, 3, 16, LANES), BF16), vm((peers, 2, 3, 16, LANES), BF16),
                vm((3, plan.nhi * SUB, LANES), F32),
                vm((plan.nhi * SUB, LANES), F32),
                vm((peers, plan.rows, LANES), BF16), vm((peers, plan.rows, LANES), BF16),
                vm((plan.half, plan.nch * cpd), BF16),
                vm((plan.nz, 2, cpd, 2 * plan.ec), BF16),
                vm((plan.half, 2 * plan.ec), F32),
                vm((plan.half, plan.ec), BF16), vm((plan.half, plan.ec), BF16),
                vm((2 * plan.ka, plan.nhi), BF16), vm((plan.nhi, 2 * plan.ka), BF16),
                vm((2, plan.ka, LANES), F32),
                vm((2 * LANES, 2 * LANES), BF16), vm((2 * LANES, 2 * LANES), BF16),
                dma((21,)), dma((2, 2, 2, hops)), dma((2, 2, 2, hops)), dma((3, 2, 2, hops)), dma((3, 2, 2, hops)),
                dma((2,)), dma((2,)), dma((3,)), dma((3,)), dma((4,)), dma((4,)),
                dma((plan.n_y + 4,)), dma((plan.n_y + 4,)), dma((3,)), dma((3,)),
            ],
            compiler_params=pltpu.CompilerParams(
                collective_id=0, has_side_effects=True, vmem_limit_bytes=56 * 1024 * 1024
            ),
            name="hyena",
        )(tokens, in_weight, spectrum, out_weight, *consts, conv_weight, skip)

    return shards


def on_mesh(mesh, plan):
    placed = (
        P("seq", "chan"),
        P(None, None, "chan"),
        P(None, None, "chan"),
        P(None, "chan", "seq", None),
        P("chan"),
        P("chan", None),
    )
    return jax.shard_map(make(plan), mesh=mesh, in_specs=placed, out_specs=P("seq", "chan"), check_vma=False)


def solution(mesh):
    return on_mesh(mesh, Plan(ns=16, nch=16, n_y=4, x_hi=2, tok=1024, ds=256, ec=256))
```

```python
import math

import jax
import jax.numpy as jnp
import numpy as np
from jax import lax
from jax.experimental import pallas as pl
from jax.experimental.pallas import tpu as pltpu
from jax.sharding import PartitionSpec as P

MESH = pl.DeviceIdType.MESH
LANES = 128
SUB = 8
BF16 = jnp.bfloat16
F32 = jnp.float32


class Plan:
    def __init__(self, ns, nch, n_y, x_hi, tok, ds, ec):
        self.ns, self.nch, self.nz, self.n_y, self.x_hi = ns, nch, nch // 2, n_y, x_hi
        self.tok, self.half, self.ds, self.ec = tok, tok // 2, ds, ec
        self.cpd = SUB * ns
        self.d, self.e = nch * ds, nch * ec
        self.nhi = ns * tok // LANES
        self.ka = 2 * self.nhi
        self.nfft = 2 * ns * tok
        self.k1 = 2 * ns
        self.m = self.ka // self.k1
        self.k2 = self.m * LANES
        self.blocks = self.half // LANES
        self.rows = self.blocks * SUB
        self.piece = self.cpd // (2 * n_y)


def tables(plan):
    m, s, k1l = np.meshgrid(np.arange(plan.m), np.arange(plan.ns), np.arange(2), indexing="ij")
    ka = (2 * s + k1l + plan.k1 * m).reshape(-1).astype(np.int64)
    nhi = np.arange(plan.nhi, dtype=np.int64)
    lane = np.arange(LANES, dtype=np.int64)

    def angle(a, b, mod):
        return (a[:, None] * b[None, :] % mod) * (2.0 * math.pi / mod)

    left = angle(ka, nhi, plan.ka)
    f1 = np.concatenate([np.cos(left), -np.sin(left)], axis=0)
    g1 = np.concatenate([np.cos(left.T), -np.sin(left.T)], axis=1) / plan.nfft
    turn = angle(ka, lane, plan.nfft)
    tw = np.stack([np.cos(turn), -np.sin(turn)])
    right = angle(lane, lane, LANES)
    c, sn = np.cos(right), np.sin(right)
    f2 = np.block([[c, -sn], [sn, c]])
    g2 = np.block([[c, sn], [-sn, c]])
    order = np.zeros((plan.k2, plan.k2), np.float32)
    k2 = np.arange(plan.k2)
    order[k2, (k2 % plan.m) * LANES + k2 // plan.m] = 1.0
    as_bf16 = lambda a: jnp.asarray(a.astype(np.float32).astype(BF16))
    return (as_bf16(f1), as_bf16(g1), jnp.asarray(tw.astype(np.float32)), as_bf16(f2), as_bf16(g2), as_bf16(order))


def kernel(
    plan, tokens, in_w, spec, out_w, f1_h, g1_h, tw_h, f2_h, g2_h, ord_h, conv_w, skip_w, out,
    w_all, tok_v, acc, spec_v, ord_v, spec_s, spec_r, spec_f, proj_s, proj_r, proj_f,
    gate_f, gate_s, gate_r, gate_a, ow, o_acc, o_own, o_far, f1, g1, tw, f2, g2,
    load_sem, ring_send, ring_recv, ring2_send, ring2_recv, x_send, x_recv, w_send, w_recv,
    a2a_send, a2a_recv, ow_send, ow_recv, out_send, out_recv,
):
    ns, nz, nch, n_y, half, ds, ec, cpd = plan.ns, plan.nz, plan.nch, plan.n_y, plan.half, plan.ds, plan.ec, plan.cpd
    s, c = lax.axis_index("seq"), lax.axis_index("chan")
    core, xh, y = lax.rem(s, 2), lax.rem(s // 2, plan.x_hi), s // (2 * plan.x_hi)
    xl, z = c // nz, lax.rem(c, nz)
    other = 1 - xl
    partner = other * nz + z
    me, here, peers = xl * ns + s, 2 * s + xl, 2 * ns
    hops = nz // 2
    part = half // 2
    wide = 3 * cpd

    def seq_of(y_, xh_, core_):
        return (y_ * plan.x_hi + xh_) * 2 + core_

    def remote(src, dst, ss, rs, seq, chan):
        return pltpu.make_async_remote_copy(
            src_ref=src, dst_ref=dst, send_sem=ss, recv_sem=rs,
            device_id={"seq": seq, "chan": chan}, device_id_type=MESH,
        )

    def arrived(ref, sem):
        pltpu.make_async_copy(ref, ref, sem).wait()

    def place(grp, off):
        k = min(off, nz - off) if isinstance(off, int) else jnp.minimum(off, nz - off)
        return 4 * k - 2 + 2 * ((nz - 1 - off) // hops) + grp

    def origin(side, at):
        grp, off = next((g, o) for g in range(2) for o in range(nz) if place(g, o) == at)
        return (side if grp == 0 else 1 - side) * nz + lax.rem(z + off, nz)

    def rows_of(block):
        return pl.ds(pl.multiple_of(block * ds, ds), ds)

    def start_weights():
        for at in range(nch):
            rows = rows_of(origin(xl, at))
            for p in range(3):
                pltpu.make_async_copy(
                    in_w.at[p, rows, :], w_all.at[at * ds : (at + 1) * ds, p * cpd : (p + 1) * cpd], load_sem.at[1]
                ).start()

    loads = [pltpu.make_async_copy(tokens.at[pl.ds(xl * half, half), :], tok_v.at[:, 0:ds], load_sem.at[0])]
    loads += [pltpu.make_async_copy(a, b, load_sem.at[2 + i]) for i, (a, b) in enumerate(
        [(ord_h, ord_v), (f1_h, f1), (g1_h, g1), (tw_h, tw), (f2_h, f2), (g2_h, g2)])]
    spec_loads = [
        pltpu.make_async_copy(spec.at[p, :, k, :], spec_v.at[p, k], load_sem.at[8 + 2 * p + k])
        for p in range(2) for k in range(2)
    ]

    def hop(by, size):
        return min(by, size - by)

    others = [(dy, dh, dl, dk) for dy in range(n_y) for dh in range(plan.x_hi) for dl in range(2) for dk in range(2)]
    others = sorted(others[1:], key=lambda o: -hop(o[0], n_y) - (2 if o[1] and not o[2] else int(bool(o[1] or o[2]))))

    def peer(o):
        dy, dh, dl, dk = o
        seq = seq_of(lax.rem(y + dy, n_y), lax.rem(xh + dh, plan.x_hi), lax.rem(core + dk, 2))
        return seq, xl if dl == 0 else other

    bar = pltpu.get_barrier_semaphore()

    for dz in range(1, nz):
        there = xl * nz + lax.rem(z + dz, nz)
        pl.semaphore_signal(bar, inc=1, device_id={"seq": s, "chan": there}, device_id_type=MESH)
    for o in reversed(others):
        seq, side = peer(o)
        pl.semaphore_signal(bar, inc=1, device_id={"seq": seq, "chan": side * nz + z}, device_id_type=MESH)
    for cp in loads[:2] + spec_loads:
        cp.start()
    start_weights()
    for cp in loads[2:]:
        cp.start()
    pl.semaphore_wait(bar, peers - 1 + nz - 1)

    reach = {(0, 0): hops, (1, 0): nz - 1 - hops, (0, 1): nz - 1 - hops, (1, 1): hops}
    sent = []

    def go(cp):
        cp.start()
        sent.append(cp)

    class Ring:
        def __init__(self, buf, width, parts, send, recv):
            self.buf, self.width, self.parts, self.send, self.recv = buf, width, parts, send, recv

        def item(self, r, way, grp, k):
            at = place(grp, (nz - k if way == 0 else k) % nz)
            lo, hi = self.parts[r]
            return self.buf.at[lo:hi, at * self.width : (at + 1) * self.width]

        def hand_on(self, r, way, grp, k, src=None):
            to = lax.rem(z + 1, nz) if way == 0 else lax.rem(z + nz - 1, nz)
            go(remote(
                self.item(r, way, grp, k) if src is None else src, self.item(r, way, grp, k + 1),
                self.send.at[r, way, grp, k], self.recv.at[r, way, grp, k], s, xl * nz + to,
            ))

        def begin(self, r, grp, src=None):
            for way in range(2):
                if reach[way, grp] > 0:
                    self.hand_on(r, way, grp, 0, src)

        def step(self, r, k):
            for grp in range(2):
                for way in range(2):
                    if k <= reach[way, grp]:
                        arrived(self.item(r, way, grp, k), self.recv.at[r, way, grp, k - 1])
                        if k < reach[way, grp]:
                            self.hand_on(r, way, grp, k)

    def token_rows(side, r):
        return tokens.at[pl.ds(pl.multiple_of(side * half + r * part, part), part), :]

    ring = Ring(tok_v, ds, [(0, part), (part, half)], ring_send, ring_recv)
    far_home = tok_v.at[:, ds : 2 * ds]

    def swap(r):
        go(remote(token_rows(other, r), far_home.at[r * part : (r + 1) * part, :], x_send.at[r], x_recv.at[r], s, partner))

    swap(0)
    ring.begin(0, 0, token_rows(xl, 0))
    swap(1)
    ring.begin(1, 0, token_rows(xl, 1))

    quarter = nch // 4

    def far_rows(i):
        q = (2 * core + i) * quarter * ds
        return pl.ds(pl.multiple_of(q, quarter * ds), quarter * ds)

    for i, xh_ in ((0, lax.rem(xh + xl, plan.x_hi)), (1, lax.rem(xh + plan.x_hi - 1 + xl, plan.x_hi))):
        for j in range(quarter):
            first, second = origin(other, i * quarter + j), origin(other, (2 + i) * quarter + j)
            rows = rows_of(first + core * (second - first))
            to = pl.ds(pl.multiple_of((2 * core + i) * quarter * ds + j * ds, ds), ds)
            for p in range(3):
                remote(
                    in_w.at[p, rows, :], w_all.at[to, wide + p * cpd : wide + (p + 1) * cpd],
                    w_send.at[i], w_recv.at[i], seq_of(y, xh_, core), partner,
                ).start()

    row = pl.ds(pl.multiple_of((core * n_y + y) * plan.piece, plan.piece), plan.piece)
    if plan.x_hi == 2:
        sides = [(xh, pl.ds(pl.multiple_of(xh * ec, ec), ec))]
    else:
        sides = [(0, pl.ds(0, ec)), (1, pl.ds(ec, ec))]

    def out_cols(g, zz):
        return pl.ds(pl.multiple_of((g * nz + zz) * ec, ec), ec)

    def ow_first(d, carry):
        zz = lax.rem(z + d, nz)
        at = place(0, nz - d) // 2
        for g, to in sides:
            remote(out_w.at[row, out_cols(g, zz)], ow.at[at, 0, row, to], ow_send.at[0], ow_recv.at[0], s, xl * nz + zz).start()
        return carry

    lax.fori_loop(1, nz, ow_first, 0)
    ow_own = [
        pltpu.make_async_copy(out_w.at[row, out_cols(g, z)], ow.at[0, 0, row, to], load_sem.at[12 + i])
        for i, (g, to) in enumerate(sides)
    ]
    for cp in ow_own:
        cp.start()

    arrived(far_home.at[0:part, :], x_recv.at[0])
    ring.begin(0, 1)

    loads[1].wait()
    for p in range(2):
        turned = []
        for k in range(2):
            spec_loads[2 * p + k].wait()
            turned.append(jnp.dot(spec_v[p, k].astype(BF16), ord_v[...], preferred_element_type=F32))
        for m in range(plan.m):
            pair = [t[:, m * LANES : (m + 1) * LANES].reshape(ns, SUB, LANES) for t in turned]
            spec_s[:, p, m] = jnp.concatenate(pair, axis=1).astype(BF16)
    spec_own = pltpu.make_async_copy(spec_s.at[s], spec_r.at[s], load_sem.at[14])
    spec_own.start()

    def send_spec(d, carry):
        q = lax.rem(s + d, ns)
        remote(spec_s.at[q], spec_r.at[s], a2a_send.at[0], a2a_recv.at[0], q, c).start()
        return carry

    lax.fori_loop(1, ns, send_spec, 0)

    def pack(value, r, g, p):
        pair = [value[i * LANES : (i + 1) * LANES, :].T.reshape(ns, SUB, LANES) for i in range(2)]
        at = xl if g == 0 else other
        proj_s[pl.ds(at * ns, ns), r, p] = jnp.concatenate(pair, axis=1).astype(BF16)

    def send_proj(r, g):
        for o in others:
            seq, side = peer(o)
            if o[2] == g:
                remote(
                    proj_s.at[side * ns + seq, r], proj_r.at[here, r], a2a_send.at[1 + r], a2a_recv.at[1 + r],
                    seq, side * nz + z,
                ).start()
        if g == 0:
            pltpu.make_async_copy(proj_s.at[me, r], proj_r.at[here, r], load_sem.at[15 + r]).start()

    def project(r, g):
        rows = slice(r * part, (r + 1) * part)
        value = jnp.dot(tok_v[rows, :], w_all[:, g * wide : (g + 1) * wide], preferred_element_type=F32)
        for p in range(3):
            pack(value[:, p * cpd : (p + 1) * cpd], r, g, p)
        send_proj(r, g)

    def ow_second():
        for cp in ow_own:
            cp.wait()
        mine = ow.at[:, 0, row, sides[0][1]] if plan.x_hi == 2 else ow.at[:, 0, row, :]
        arrived(mine.at[0 : nz - 1], ow_recv.at[0])
        far = ow.at[:, 1, row, sides[0][1]] if plan.x_hi == 2 else ow.at[:, 1, row, :]
        go(remote(mine, far, ow_send.at[1], ow_recv.at[1], s, partner))
        if plan.x_hi == 2:
            go(remote(mine, mine, ow_send.at[2], ow_recv.at[2], seq_of(y, 1 - xh, core), c))
            go(remote(mine, far, ow_send.at[3], ow_recv.at[3], seq_of(y, 1 - xh, core), partner))

    def ow_third():
        if plan.x_hi == 2:
            away = pl.ds(pl.multiple_of((1 - xh) * ec, ec), ec)
            arrived(ow.at[:, 1, row, sides[0][1]], ow_recv.at[1])
            arrived(ow.at[:, 0, row, away], ow_recv.at[2])
            arrived(ow.at[:, 1, row, away], ow_recv.at[3])
        else:
            arrived(ow.at[:, 1, row, :], ow_recv.at[1])
        for dy in range(1, n_y):
            go(remote(ow.at[:, :, row, :], ow.at[:, :, row, :], ow_send.at[3 + dy], ow_recv.at[3 + dy],
                      seq_of(lax.rem(y + dy, n_y), xh, core), c))

    half_ow = n_y * plan.piece

    def ow_fourth():
        for dy in range(1, n_y):
            yy = lax.rem(y + n_y - dy, n_y)
            piece = pl.ds(pl.multiple_of((core * n_y + yy) * plan.piece, plan.piece), plan.piece)
            arrived(ow.at[:, :, piece, :], ow_recv.at[3 + dy])
        side = pl.ds(pl.multiple_of(core * half_ow, half_ow), half_ow)
        go(remote(ow.at[:, :, side, :], ow.at[:, :, side, :], ow_send.at[3 + n_y], ow_recv.at[3 + n_y], seq_of(y, xh, 1 - core), c))

    def ow_last():
        away = pl.ds(pl.multiple_of((1 - core) * half_ow, half_ow), half_ow)
        arrived(ow.at[:, :, away, :], ow_recv.at[3 + n_y])

    def far_pass():
        for i in range(2):
            arrived(w_all.at[far_rows(i), wide : 2 * wide], w_recv.at[i])
        side = pl.ds(pl.multiple_of(core * 2 * quarter * ds, 2 * quarter * ds), 2 * quarter * ds)
        mine = w_all.at[side, wide : 2 * wide]
        go(remote(mine, mine, w_send.at[2], w_recv.at[2], seq_of(y, xh, 1 - core), c))

    def far_wait():
        away = pl.ds(pl.multiple_of((1 - core) * 2 * quarter * ds, 2 * quarter * ds), 2 * quarter * ds)
        arrived(w_all.at[away, wide : 2 * wide], w_recv.at[2])

    def own_wait():
        loads[0].wait()
        arrived(w_all.at[:, 0:wide], load_sem.at[1])

    def begin_second():
        arrived(far_home.at[part : 2 * part, :], x_recv.at[1])
        ring.begin(1, 1)

    bulk = (nch - 2) * ds
    rows = slice(part, 2 * part)

    def bulk_second():
        for at in range(0, 2 * wide, 2 * cpd):
            acc[:, at : at + 2 * cpd] = jnp.dot(
                tok_v[rows, 0:bulk], w_all[0:bulk, at : at + 2 * cpd], preferred_element_type=F32)

    after = {}
    steps = sorted((k + r * (hops - 1.5), r, k) for r in range(2) for k in range(1, hops + 1))
    place_of = {(r, k): i for i, (_, r, k) in enumerate(steps)}

    def hook(r, k, *does):
        k = max(1, min(k, hops))
        after.setdefault(place_of[r, k], []).extend(does)

    hook(0, 2, begin_second)
    hook(1, 1, ow_second)
    hook(0, hops, own_wait, lambda: project(0, 0))
    hook(1, 2, far_pass)
    hook(1, hops - 1, far_wait, lambda: project(0, 1), bulk_second)
    for i, (_, r, k) in enumerate(steps):
        ring.step(r, k)
        for do in after.get(i, []):
            do()
    rest = acc[...] + jnp.dot(tok_v[rows, bulk:], w_all[bulk:, :], preferred_element_type=F32)
    for g in range(2):
        for p in range(3):
            at = g * wide + p * cpd
            pack(rest[:, at : at + cpd], 1, g, p)
        send_proj(1, g)

    spec_own.wait()
    arrived(spec_r.at[0 : ns - 1], a2a_recv.at[0])

    def lay(i, carry):
        for p in range(2):
            for m in range(plan.m):
                spec_f[p, pl.ds(pl.multiple_of((m * ns + i) * 16, 16), 16), :] = spec_r[i, p, m].astype(F32)
        return carry

    lax.fori_loop(0, ns, lay, 0)
    for cp in loads[2:]:
        cp.wait()
    for r in range(2):
        arrived(proj_r.at[here, r], load_sem.at[15 + r])
        arrived(proj_r.at[0 : peers - 1, r], a2a_recv.at[1 + r])
        for p in range(3):
            for q in range(peers):
                proj_f[p, q * plan.rows + 16 * r : q * plan.rows + 16 * (r + 1), :] = proj_r[q, r, p].astype(F32)

    lane = lax.broadcasted_iota(jnp.int32, (plan.nhi, LANES), 1)
    posn = lane + LANES * lax.broadcasted_iota(jnp.int32, (plan.nhi, LANES), 0)

    def behind(x, by):
        turned = pltpu.roll(x, by, 1)
        both = jnp.where(lane < by, pltpu.roll(turned, 1, 0), turned)
        return jnp.where(posn < by, 0.0, both)

    def transform(ch, carry):
        chan = s * SUB + ch
        parts = []
        for p in range(3):
            x = proj_f[p, pl.ds(ch, plan.nhi, stride=SUB), :]
            f = conv_w[0, p, chan] * x
            for j in range(1, 3):
                f = f + conv_w[j, p, chan] * behind(x, j)
            parts.append(f)
        query, signal = parts[0], (parts[1] * parts[2]).astype(BF16)
        a = jnp.dot(f1[...], signal, preferred_element_type=F32)
        ar, ai = a[: plan.ka], a[plan.ka :]
        tr, ti = tw[0], tw[1]
        yy = jnp.concatenate([(ar * tr - ai * ti).astype(BF16), (ar * ti + ai * tr).astype(BF16)], axis=1)
        zz = jnp.dot(yy, f2[...], preferred_element_type=F32)
        zr, zi = zz[:, :LANES], zz[:, LANES:]
        hr, hi = (spec_f[p, pl.ds(ch, plan.ka, stride=SUB), :] for p in range(2))
        pp = jnp.concatenate([(zr * hr - zi * hi).astype(BF16), (zr * hi + zi * hr).astype(BF16)], axis=1)
        u = jnp.dot(pp, g2[...], preferred_element_type=F32)
        ur, ui = u[:, :LANES], u[:, LANES:]
        v = jnp.concatenate([(ur * tr + ui * ti).astype(BF16), (ui * tr - ur * ti).astype(BF16)], axis=0)
        longconv = jnp.dot(g1[...], v, preferred_element_type=F32)
        gate_f[pl.ds(ch, plan.nhi, stride=SUB), :] = query * (longconv + skip_w[chan] * signal.astype(F32))
        return carry

    lax.fori_loop(0, SUB, transform, 0, unroll=True)
    gate_s[...] = gate_f[...].astype(BF16).reshape(peers, plan.rows, LANES)

    for o in others:
        seq, side = peer(o)
        remote(gate_s.at[2 * seq + side], gate_r.at[me], a2a_send.at[3], a2a_recv.at[3], seq, side * nz + z).start()
    gate_own = pltpu.make_async_copy(gate_s.at[here], gate_r.at[me], load_sem.at[17])
    gate_own.start()
    gate_own.wait()
    arrived(gate_r.at[0 : peers - 1], a2a_recv.at[3])

    n_parts = 4
    parts2 = [(i * half // n_parts, (i + 1) * half // n_parts) for i in range(n_parts)]
    ring2 = Ring(gate_a, cpd, parts2, ring2_send, ring2_recv)

    def repack(r):
        lo, hi = parts2[r]
        for grp in range(2):
            for j in range(lo // LANES, hi // LANES):
                rows = gate_r[pl.ds((xl if grp == 0 else other) * ns, ns), 16 * (j // 2) : 16 * (j // 2 + 1), :].astype(F32)
                block = rows[:, SUB * (j % 2) : SUB * (j % 2 + 1), :].reshape(cpd, LANES)
                gate_a[j * LANES : (j + 1) * LANES, grp * cpd : (grp + 1) * cpd] = block.T.astype(BF16)
            ring2.begin(r, grp)

    k_bulk = (nch - 2) * cpd

    def weights(lo, hi):
        return ow[lo // (2 * cpd) : hi // (2 * cpd)].reshape(hi - lo, 2 * ec)

    def mix():
        o_acc[...] = jnp.dot(gate_a[:, 0:k_bulk], weights(0, k_bulk), preferred_element_type=F32)

    def own_rows(side, r):
        lo, hi = parts2[r]
        return out.at[pl.ds(pl.multiple_of(side * half + lo, LANES), hi - lo), :]

    def finish(r):
        lo, hi = parts2[r]
        total = o_acc[lo:hi, :] + jnp.dot(gate_a[lo:hi, k_bulk:], weights(k_bulk, nch * cpd), preferred_element_type=F32)
        left, right = total[:, :ec].astype(BF16), total[:, ec:].astype(BF16)
        o_far[lo:hi, :] = jnp.where(xl == 0, right, left)
        go(remote(o_far.at[lo:hi, :], own_rows(xl, r), out_send.at[r], out_recv.at[r], s, partner))
        o_own[lo:hi, :] = jnp.where(xl == 0, left, right)
        pltpu.make_async_copy(o_own.at[lo:hi, :], own_rows(xl, r), load_sem.at[18 + r]).start()

    ow_third()
    repack(0)
    for r in range(1, n_parts):
        repack(r)
    for k in range(1, hops):
        for r in range(n_parts):
            ring2.step(r, k)
            if (k, r) == (max(hops - 2, 1), 3):
                ow_fourth()
    ow_last()
    mix()
    for r in range(n_parts):
        ring2.step(r, hops)
        finish(r)

    for cp in sent:
        cp.wait_send()
    for i in range(2):
        arrived(w_all.at[0 : quarter * ds, wide : 2 * wide], w_send.at[i])
        arrived(proj_s.at[0 : peers - 1, i], a2a_send.at[1 + i])
    arrived(spec_s.at[0 : ns - 1], a2a_send.at[0])
    arrived(gate_s.at[0 : peers - 1], a2a_send.at[3])
    legs = ow.at[0 : nz - 1, 0, row, sides[0][1]] if plan.x_hi == 2 else ow.at[0 : nz - 1, 0, row, :]
    arrived(legs, ow_send.at[0])
    for r in range(n_parts):
        arrived(own_rows(xl, r), load_sem.at[18 + r])
        arrived(own_rows(other, r), out_recv.at[r])


def make(plan):
    consts = tables(plan)

    def shards(tokens, in_weight, conv_weight, spectrum, skip, out_weight):
        ns, peers, cpd = plan.ns, 2 * plan.ns, plan.cpd
        hops = plan.nz // 2
        vm = pltpu.VMEM
        dma = pltpu.SemaphoreType.DMA
        anywhere = pl.BlockSpec(memory_space=pl.ANY)
        scalars = pl.BlockSpec(memory_space=pltpu.SMEM)
        return pl.pallas_call(
            lambda *refs: kernel(plan, *refs),
            out_shape=jax.ShapeDtypeStruct((plan.tok, plan.ec), BF16),
            in_specs=[anywhere] * 10 + [scalars] * 2,
            out_specs=anywhere,
            scratch_shapes=[
                vm((plan.d, 6 * cpd), BF16),
                vm((plan.half, plan.d), BF16),
                vm((plan.half // 2, 6 * cpd), F32),
                vm((2, 2, cpd, plan.k2), F32), vm((plan.k2, plan.k2), BF16),
                vm((ns, 2, plan.m, 16, LANES), BF16), vm((ns, 2, plan.m, 16, LANES), BF16),
                vm((2, plan.m * ns * 16, LANES), F32),
                vm((peers, 2, 3, 16, LANES), BF16), vm((peers, 2, 3, 16, LANES), BF16),
                vm((3, plan.nhi * SUB, LANES), F32),
                vm((plan.nhi * SUB, LANES), F32),
                vm((peers, plan.rows, LANES), BF16), vm((peers, plan.rows, LANES), BF16),
                vm((plan.half, plan.nch * cpd), BF16),
                vm((plan.nz, 2, cpd, 2 * plan.ec), BF16),
                vm((plan.half, 2 * plan.ec), F32),
                vm((plan.half, plan.ec), BF16), vm((plan.half, plan.ec), BF16),
                vm((2 * plan.ka, plan.nhi), BF16), vm((plan.nhi, 2 * plan.ka), BF16),
                vm((2, plan.ka, LANES), F32),
                vm((2 * LANES, 2 * LANES), BF16), vm((2 * LANES, 2 * LANES), BF16),
                dma((22,)), dma((2, 2, 2, hops)), dma((2, 2, 2, hops)), dma((4, 2, 2, hops)), dma((4, 2, 2, hops)),
                dma((2,)), dma((2,)), dma((3,)), dma((3,)), dma((4,)), dma((4,)),
                dma((plan.n_y + 4,)), dma((plan.n_y + 4,)), dma((4,)), dma((4,)),
            ],
            compiler_params=pltpu.CompilerParams(
                collective_id=0, has_side_effects=True, vmem_limit_bytes=56 * 1024 * 1024
            ),
            name="hyena",
        )(tokens, in_weight, spectrum, out_weight, *consts, conv_weight, skip)

    return shards


def on_mesh(mesh, plan):
    placed = (
        P("seq", "chan"),
        P(None, None, "chan"),
        P(None, None, "chan"),
        P(None, "chan", "seq", None),
        P("chan"),
        P("chan", None),
    )
    return jax.shard_map(make(plan), mesh=mesh, in_specs=placed, out_specs=P("seq", "chan"), check_vma=False)


def solution(mesh):
    return on_mesh(mesh, Plan(ns=16, nch=16, n_y=4, x_hi=2, tok=1024, ds=256, ec=256))
```

```python
import math

import jax
import jax.numpy as jnp
import numpy as np
from jax import lax
from jax.experimental import pallas as pl
from jax.experimental.pallas import tpu as pltpu
from jax.sharding import PartitionSpec as P

MESH = pl.DeviceIdType.MESH
LANES = 128
SUB = 8
BF16 = jnp.bfloat16
F32 = jnp.float32


class Plan:
    def __init__(self, ns, nch, n_y, x_hi, tok, ds, ec):
        self.ns, self.nch, self.nz, self.n_y, self.x_hi = ns, nch, nch // 2, n_y, x_hi
        self.tok, self.half, self.ds, self.ec = tok, tok // 2, ds, ec
        self.cpd = SUB * ns
        self.d, self.e = nch * ds, nch * ec
        self.nhi = ns * tok // LANES
        self.ka = 2 * self.nhi
        self.nfft = 2 * ns * tok
        self.k1 = 2 * ns
        self.m = self.ka // self.k1
        self.k2 = self.m * LANES
        self.blocks = self.half // LANES
        self.rows = self.blocks * SUB
        self.piece = self.cpd // (2 * n_y)


def tables(plan):
    m, s, k1l = np.meshgrid(np.arange(plan.m), np.arange(plan.ns), np.arange(2), indexing="ij")
    ka = (2 * s + k1l + plan.k1 * m).reshape(-1).astype(np.int64)
    nhi = np.arange(plan.nhi, dtype=np.int64)
    lane = np.arange(LANES, dtype=np.int64)

    def angle(a, b, mod):
        return (a[:, None] * b[None, :] % mod) * (2.0 * math.pi / mod)

    left = angle(ka, nhi, plan.ka)
    f1 = np.concatenate([np.cos(left), -np.sin(left)], axis=0)
    g1 = np.concatenate([np.cos(left.T), -np.sin(left.T)], axis=1) / plan.nfft
    turn = angle(ka, lane, plan.nfft)
    tw = np.stack([np.cos(turn), -np.sin(turn)])
    right = angle(lane, lane, LANES)
    c, sn = np.cos(right), np.sin(right)
    f2 = np.block([[c, -sn], [sn, c]])
    g2 = np.block([[c, sn], [-sn, c]])
    order = np.zeros((plan.k2, plan.k2), np.float32)
    k2 = np.arange(plan.k2)
    order[k2, (k2 % plan.m) * LANES + k2 // plan.m] = 1.0
    as_bf16 = lambda a: jnp.asarray(a.astype(np.float32).astype(BF16))
    return (as_bf16(f1), as_bf16(g1), jnp.asarray(tw.astype(np.float32)), as_bf16(f2), as_bf16(g2), as_bf16(order))


def kernel(
    plan, tokens, in_w, spec, out_w, f1_h, g1_h, tw_h, f2_h, g2_h, ord_h, conv_w, skip_w, out,
    w_all, tok_v, acc, spec_v, ord_v, spec_s, spec_r, spec_f, proj_s, proj_r, proj_f,
    gate_f, gate_s, gate_r, gate_a, ow, o_acc, o_own, o_far, f1, g1, tw, f2, g2,
    load_sem, ring_send, ring_recv, ring2_send, ring2_recv, x_send, x_recv, w_send, w_recv,
    a2a_send, a2a_recv, ow_send, ow_recv, out_send, out_recv,
):
    ns, nz, nch, n_y, half, ds, ec, cpd = plan.ns, plan.nz, plan.nch, plan.n_y, plan.half, plan.ds, plan.ec, plan.cpd
    s, c = lax.axis_index("seq"), lax.axis_index("chan")
    core, xh, y = lax.rem(s, 2), lax.rem(s // 2, plan.x_hi), s // (2 * plan.x_hi)
    xl, z = c // nz, lax.rem(c, nz)
    other = 1 - xl
    partner = other * nz + z
    me, here, peers = xl * ns + s, 2 * s + xl, 2 * ns
    hops = nz // 2
    part = half // 2
    wide = 3 * cpd

    def seq_of(y_, xh_, core_):
        return (y_ * plan.x_hi + xh_) * 2 + core_

    def remote(src, dst, ss, rs, seq, chan):
        return pltpu.make_async_remote_copy(
            src_ref=src, dst_ref=dst, send_sem=ss, recv_sem=rs,
            device_id={"seq": seq, "chan": chan}, device_id_type=MESH,
        )

    def arrived(ref, sem):
        pltpu.make_async_copy(ref, ref, sem).wait()

    def place(grp, off):
        k = min(off, nz - off) if isinstance(off, int) else jnp.minimum(off, nz - off)
        return 4 * k - 2 + 2 * ((nz - 1 - off) // hops) + grp

    def origin(side, at):
        grp, off = next((g, o) for g in range(2) for o in range(nz) if place(g, o) == at)
        return (side if grp == 0 else 1 - side) * nz + lax.rem(z + off, nz)

    def rows_of(block):
        return pl.ds(pl.multiple_of(block * ds, ds), ds)

    def start_weights():
        for at in range(nch):
            rows = rows_of(origin(xl, at))
            for p in range(3):
                pltpu.make_async_copy(
                    in_w.at[p, rows, :], w_all.at[at * ds : (at + 1) * ds, p * cpd : (p + 1) * cpd], load_sem.at[1]
                ).start()

    loads = [pltpu.make_async_copy(tokens.at[pl.ds(xl * half, half), :], tok_v.at[:, 0:ds], load_sem.at[0])]
    loads += [pltpu.make_async_copy(a, b, load_sem.at[2 + i]) for i, (a, b) in enumerate(
        [(ord_h, ord_v), (f1_h, f1), (g1_h, g1), (tw_h, tw), (f2_h, f2), (g2_h, g2)])]
    spec_loads = [
        pltpu.make_async_copy(spec.at[p, :, k, :], spec_v.at[p, k], load_sem.at[8 + 2 * p + k])
        for p in range(2) for k in range(2)
    ]

    def hop(by, size):
        return min(by, size - by)

    others = [(dy, dh, dl, dk) for dy in range(n_y) for dh in range(plan.x_hi) for dl in range(2) for dk in range(2)]
    others = sorted(others[1:], key=lambda o: -hop(o[0], n_y) - (2 if o[1] and not o[2] else int(bool(o[1] or o[2]))))

    def peer(o):
        dy, dh, dl, dk = o
        seq = seq_of(lax.rem(y + dy, n_y), lax.rem(xh + dh, plan.x_hi), lax.rem(core + dk, 2))
        return seq, xl if dl == 0 else other

    bar = pltpu.get_barrier_semaphore()

    for dz in range(1, nz):
        there = xl * nz + lax.rem(z + dz, nz)
        pl.semaphore_signal(bar, inc=1, device_id={"seq": s, "chan": there}, device_id_type=MESH)
    for o in reversed(others):
        seq, side = peer(o)
        pl.semaphore_signal(bar, inc=1, device_id={"seq": seq, "chan": side * nz + z}, device_id_type=MESH)
    for cp in loads[:2] + spec_loads:
        cp.start()
    start_weights()
    for cp in loads[2:]:
        cp.start()
    pl.semaphore_wait(bar, peers - 1 + nz - 1)

    reach = {(0, 0): hops, (1, 0): nz - 1 - hops, (0, 1): nz - 1 - hops, (1, 1): hops}
    sent = []

    def go(cp):
        cp.start()
        sent.append(cp)

    class Ring:
        def __init__(self, buf, width, parts, send, recv):
            self.buf, self.width, self.parts, self.send, self.recv = buf, width, parts, send, recv

        def item(self, r, way, grp, k):
            at = place(grp, (nz - k if way == 0 else k) % nz)
            lo, hi = self.parts[r]
            return self.buf.at[lo:hi, at * self.width : (at + 1) * self.width]

        def hand_on(self, r, way, grp, k, src=None):
            to = lax.rem(z + 1, nz) if way == 0 else lax.rem(z + nz - 1, nz)
            go(remote(
                self.item(r, way, grp, k) if src is None else src, self.item(r, way, grp, k + 1),
                self.send.at[r, way, grp, k], self.recv.at[r, way, grp, k], s, xl * nz + to,
            ))

        def begin(self, r, grp, src=None):
            for way in range(2):
                if reach[way, grp] > 0:
                    self.hand_on(r, way, grp, 0, src)

        def step(self, r, k):
            for grp in range(2):
                for way in range(2):
                    if k <= reach[way, grp]:
                        arrived(self.item(r, way, grp, k), self.recv.at[r, way, grp, k - 1])
                        if k < reach[way, grp]:
                            self.hand_on(r, way, grp, k)

    def token_rows(side, r):
        return tokens.at[pl.ds(pl.multiple_of(side * half + r * part, part), part), :]

    ring = Ring(tok_v, ds, [(0, part), (part, half)], ring_send, ring_recv)
    far_home = tok_v.at[:, ds : 2 * ds]

    def swap(r):
        go(remote(token_rows(other, r), far_home.at[r * part : (r + 1) * part, :], x_send.at[r], x_recv.at[r], s, partner))

    swap(0)
    ring.begin(0, 0, token_rows(xl, 0))
    swap(1)
    ring.begin(1, 0, token_rows(xl, 1))

    quarter = nch // 4

    def far_rows(i):
        q = (2 * core + i) * quarter * ds
        return pl.ds(pl.multiple_of(q, quarter * ds), quarter * ds)

    for i, xh_ in ((0, lax.rem(xh + xl, plan.x_hi)), (1, lax.rem(xh + plan.x_hi - 1 + xl, plan.x_hi))):
        for j in range(quarter):
            first, second = origin(other, i * quarter + j), origin(other, (2 + i) * quarter + j)
            rows = rows_of(first + core * (second - first))
            to = pl.ds(pl.multiple_of((2 * core + i) * quarter * ds + j * ds, ds), ds)
            for p in range(3):
                remote(
                    in_w.at[p, rows, :], w_all.at[to, wide + p * cpd : wide + (p + 1) * cpd],
                    w_send.at[i], w_recv.at[i], seq_of(y, xh_, core), partner,
                ).start()

    row = pl.ds(pl.multiple_of((core * n_y + y) * plan.piece, plan.piece), plan.piece)
    if plan.x_hi == 2:
        sides = [(xh, pl.ds(pl.multiple_of(xh * ec, ec), ec))]
    else:
        sides = [(0, pl.ds(0, ec)), (1, pl.ds(ec, ec))]

    def out_cols(g, zz):
        return pl.ds(pl.multiple_of((g * nz + zz) * ec, ec), ec)

    def ow_first(d, carry):
        zz = lax.rem(z + d, nz)
        at = place(0, nz - d) // 2
        for g, to in sides:
            remote(out_w.at[row, out_cols(g, zz)], ow.at[at, 0, row, to], ow_send.at[0], ow_recv.at[0], s, xl * nz + zz).start()
        return carry

    lax.fori_loop(1, nz, ow_first, 0)
    ow_own = [
        pltpu.make_async_copy(out_w.at[row, out_cols(g, z)], ow.at[0, 0, row, to], load_sem.at[12 + i])
        for i, (g, to) in enumerate(sides)
    ]
    for cp in ow_own:
        cp.start()

    arrived(far_home.at[0:part, :], x_recv.at[0])
    ring.begin(0, 1)

    loads[1].wait()
    for p in range(2):
        turned = []
        for k in range(2):
            spec_loads[2 * p + k].wait()
            turned.append(jnp.dot(spec_v[p, k].astype(BF16), ord_v[...], preferred_element_type=F32))
        for m in range(plan.m):
            pair = [t[:, m * LANES : (m + 1) * LANES].reshape(ns, SUB, LANES) for t in turned]
            spec_s[:, p, m] = jnp.concatenate(pair, axis=1).astype(BF16)
    spec_own = pltpu.make_async_copy(spec_s.at[s], spec_r.at[s], load_sem.at[14])
    spec_own.start()

    def send_spec(d, carry):
        q = lax.rem(s + d, ns)
        remote(spec_s.at[q], spec_r.at[s], a2a_send.at[0], a2a_recv.at[0], q, c).start()
        return carry

    lax.fori_loop(1, ns, send_spec, 0)

    def pack(value, r, g, p):
        pair = [value[i * LANES : (i + 1) * LANES, :].T.reshape(ns, SUB, LANES) for i in range(2)]
        at = xl if g == 0 else other
        proj_s[pl.ds(at * ns, ns), r, p] = jnp.concatenate(pair, axis=1).astype(BF16)

    def send_proj(r, g):
        for o in others:
            seq, side = peer(o)
            if o[2] == g:
                remote(
                    proj_s.at[side * ns + seq, r], proj_r.at[here, r], a2a_send.at[1 + r], a2a_recv.at[1 + r],
                    seq, side * nz + z,
                ).start()
        if g == 0:
            pltpu.make_async_copy(proj_s.at[me, r], proj_r.at[here, r], load_sem.at[15 + r]).start()

    def project(r, g):
        rows = slice(r * part, (r + 1) * part)
        value = jnp.dot(tok_v[rows, :], w_all[:, g * wide : (g + 1) * wide], preferred_element_type=F32)
        for p in range(3):
            pack(value[:, p * cpd : (p + 1) * cpd], r, g, p)
        send_proj(r, g)

    def ow_second():
        for cp in ow_own:
            cp.wait()
        mine = ow.at[:, 0, row, sides[0][1]] if plan.x_hi == 2 else ow.at[:, 0, row, :]
        arrived(mine.at[0 : nz - 1], ow_recv.at[0])
        far = ow.at[:, 1, row, sides[0][1]] if plan.x_hi == 2 else ow.at[:, 1, row, :]
        go(remote(mine, far, ow_send.at[1], ow_recv.at[1], s, partner))
        if plan.x_hi == 2:
            go(remote(mine, mine, ow_send.at[2], ow_recv.at[2], seq_of(y, 1 - xh, core), c))
            go(remote(mine, far, ow_send.at[3], ow_recv.at[3], seq_of(y, 1 - xh, core), partner))

    def ow_third():
        if plan.x_hi == 2:
            away = pl.ds(pl.multiple_of((1 - xh) * ec, ec), ec)
            arrived(ow.at[:, 1, row, sides[0][1]], ow_recv.at[1])
            arrived(ow.at[:, 0, row, away], ow_recv.at[2])
            arrived(ow.at[:, 1, row, away], ow_recv.at[3])
        else:
            arrived(ow.at[:, 1, row, :], ow_recv.at[1])
        for dy in range(1, n_y):
            go(remote(ow.at[:, :, row, :], ow.at[:, :, row, :], ow_send.at[3 + dy], ow_recv.at[3 + dy],
                      seq_of(lax.rem(y + dy, n_y), xh, core), c))

    half_ow = n_y * plan.piece

    def ow_fourth():
        for dy in range(1, n_y):
            yy = lax.rem(y + n_y - dy, n_y)
            piece = pl.ds(pl.multiple_of((core * n_y + yy) * plan.piece, plan.piece), plan.piece)
            arrived(ow.at[:, :, piece, :], ow_recv.at[3 + dy])
        side = pl.ds(pl.multiple_of(core * half_ow, half_ow), half_ow)
        go(remote(ow.at[:, :, side, :], ow.at[:, :, side, :], ow_send.at[3 + n_y], ow_recv.at[3 + n_y], seq_of(y, xh, 1 - core), c))

    def ow_last():
        away = pl.ds(pl.multiple_of((1 - core) * half_ow, half_ow), half_ow)
        arrived(ow.at[:, :, away, :], ow_recv.at[3 + n_y])

    def far_pass():
        for i in range(2):
            arrived(w_all.at[far_rows(i), wide : 2 * wide], w_recv.at[i])
        side = pl.ds(pl.multiple_of(core * 2 * quarter * ds, 2 * quarter * ds), 2 * quarter * ds)
        mine = w_all.at[side, wide : 2 * wide]
        go(remote(mine, mine, w_send.at[2], w_recv.at[2], seq_of(y, xh, 1 - core), c))

    def far_wait():
        away = pl.ds(pl.multiple_of((1 - core) * 2 * quarter * ds, 2 * quarter * ds), 2 * quarter * ds)
        arrived(w_all.at[away, wide : 2 * wide], w_recv.at[2])

    def own_wait():
        loads[0].wait()
        arrived(w_all.at[:, 0:wide], load_sem.at[1])

    def begin_second():
        arrived(far_home.at[part : 2 * part, :], x_recv.at[1])
        ring.begin(1, 1)

    bulk = (nch - 2) * ds
    rows = slice(part, 2 * part)

    def bulk_second():
        for at in range(0, 2 * wide, 2 * cpd):
            acc[:, at : at + 2 * cpd] = jnp.dot(
                tok_v[rows, 0:bulk], w_all[0:bulk, at : at + 2 * cpd], preferred_element_type=F32)

    after = {}
    steps = sorted((k + r * (hops - 1.5), r, k) for r in range(2) for k in range(1, hops + 1))
    place_of = {(r, k): i for i, (_, r, k) in enumerate(steps)}

    def hook(r, k, *does):
        k = max(1, min(k, hops))
        after.setdefault(place_of[r, k], []).extend(does)

    hook(0, 2, begin_second)
    hook(1, 1, ow_second)
    hook(0, hops, own_wait, lambda: project(0, 0))
    hook(1, 2, far_pass)
    hook(1, hops - 1, far_wait, lambda: project(0, 1), bulk_second)
    for i, (_, r, k) in enumerate(steps):
        ring.step(r, k)
        for do in after.get(i, []):
            do()
    rest = acc[...] + jnp.dot(tok_v[rows, bulk:], w_all[bulk:, :], preferred_element_type=F32)
    for g in range(2):
        for p in range(3):
            at = g * wide + p * cpd
            pack(rest[:, at : at + cpd], 1, g, p)
        send_proj(1, g)

    spec_own.wait()
    arrived(spec_r.at[0 : ns - 1], a2a_recv.at[0])

    def lay(i, carry):
        for p in range(2):
            for m in range(plan.m):
                spec_f[p, pl.ds(pl.multiple_of((m * ns + i) * 16, 16), 16), :] = spec_r[i, p, m].astype(F32)
        return carry

    lax.fori_loop(0, ns, lay, 0)
    for cp in loads[2:]:
        cp.wait()
    for r in range(2):
        arrived(proj_r.at[here, r], load_sem.at[15 + r])
        arrived(proj_r.at[0 : peers - 1, r], a2a_recv.at[1 + r])
        for p in range(3):
            for q in range(peers):
                proj_f[p, q * plan.rows + 16 * r : q * plan.rows + 16 * (r + 1), :] = proj_r[q, r, p].astype(F32)

    lane = lax.broadcasted_iota(jnp.int32, (plan.nhi, LANES), 1)
    posn = lane + LANES * lax.broadcasted_iota(jnp.int32, (plan.nhi, LANES), 0)

    def behind(x, by):
        turned = pltpu.roll(x, by, 1)
        both = jnp.where(lane < by, pltpu.roll(turned, 1, 0), turned)
        return jnp.where(posn < by, 0.0, both)

    def streams(ch):
        parts = []
        for p in range(3):
            x = proj_f[p, pl.ds(ch, plan.nhi, stride=SUB), :]
            f = conv_w[0, p, s * SUB + ch] * x
            for j in range(1, 3):
                f = f + conv_w[j, p, s * SUB + ch] * behind(x, j)
            parts.append(f)
        return parts[0], (parts[1] * parts[2]).astype(BF16)

    def middle(ch, a):
        ar, ai = a[: plan.ka], a[plan.ka :]
        tr, ti = tw[0], tw[1]
        yy = jnp.concatenate([(ar * tr - ai * ti).astype(BF16), (ar * ti + ai * tr).astype(BF16)], axis=1)
        zz = jnp.dot(yy, f2[...], preferred_element_type=F32)
        zr, zi = zz[:, :LANES], zz[:, LANES:]
        hr, hi = (spec_f[p, pl.ds(ch, plan.ka, stride=SUB), :] for p in range(2))
        pp = jnp.concatenate([(zr * hr - zi * hi).astype(BF16), (zr * hi + zi * hr).astype(BF16)], axis=1)
        u = jnp.dot(pp, g2[...], preferred_element_type=F32)
        ur, ui = u[:, :LANES], u[:, LANES:]
        return jnp.concatenate([(ur * tr + ui * ti).astype(BF16), (ui * tr - ur * ti).astype(BF16)], axis=0)

    for ch in range(0, SUB, 2):
        both = [streams(ch + i) for i in range(2)]
        a = jnp.dot(f1[...], jnp.concatenate([signal for _, signal in both], axis=1), preferred_element_type=F32)
        v = jnp.concatenate([middle(ch + i, a[:, i * LANES : (i + 1) * LANES]) for i in range(2)], axis=1)
        longconv = jnp.dot(g1[...], v, preferred_element_type=F32)
        for i, (query, signal) in enumerate(both):
            direct = skip_w[s * SUB + ch + i] * signal.astype(F32)
            gate_f[pl.ds(ch + i, plan.nhi, stride=SUB), :] = query * (longconv[:, i * LANES : (i + 1) * LANES] + direct)

    gate_s[...] = gate_f[...].astype(BF16).reshape(peers, plan.rows, LANES)

    for o in others:
        seq, side = peer(o)
        remote(gate_s.at[2 * seq + side], gate_r.at[me], a2a_send.at[3], a2a_recv.at[3], seq, side * nz + z).start()
    gate_own = pltpu.make_async_copy(gate_s.at[here], gate_r.at[me], load_sem.at[17])
    gate_own.start()
    gate_own.wait()
    arrived(gate_r.at[0 : peers - 1], a2a_recv.at[3])

    n_parts = 4
    parts2 = [(i * half // n_parts, (i + 1) * half // n_parts) for i in range(n_parts)]
    ring2 = Ring(gate_a, cpd, parts2, ring2_send, ring2_recv)

    def repack(r):
        lo, hi = parts2[r]
        for grp in range(2):
            for j in range(lo // LANES, hi // LANES):
                rows = gate_r[pl.ds((xl if grp == 0 else other) * ns, ns), 16 * (j // 2) : 16 * (j // 2 + 1), :].astype(F32)
                block = rows[:, SUB * (j % 2) : SUB * (j % 2 + 1), :].reshape(cpd, LANES)
                gate_a[j * LANES : (j + 1) * LANES, grp * cpd : (grp + 1) * cpd] = block.T.astype(BF16)
            ring2.begin(r, grp)

    k_bulk = (nch - 2) * cpd

    def weights(lo, hi):
        return ow[lo // (2 * cpd) : hi // (2 * cpd)].reshape(hi - lo, 2 * ec)

    def mix():
        o_acc[...] = jnp.dot(gate_a[:, 0:k_bulk], weights(0, k_bulk), preferred_element_type=F32)

    def own_rows(side, r):
        lo, hi = parts2[r]
        return out.at[pl.ds(pl.multiple_of(side * half + lo, LANES), hi - lo), :]

    def finish(r):
        lo, hi = parts2[r]
        total = o_acc[lo:hi, :] + jnp.dot(gate_a[lo:hi, k_bulk:], weights(k_bulk, nch * cpd), preferred_element_type=F32)
        left, right = total[:, :ec].astype(BF16), total[:, ec:].astype(BF16)
        o_far[lo:hi, :] = jnp.where(xl == 0, right, left)
        go(remote(o_far.at[lo:hi, :], own_rows(xl, r), out_send.at[r], out_recv.at[r], s, partner))
        o_own[lo:hi, :] = jnp.where(xl == 0, left, right)
        pltpu.make_async_copy(o_own.at[lo:hi, :], own_rows(xl, r), load_sem.at[18 + r]).start()

    ow_third()
    repack(0)
    for r in range(1, n_parts):
        repack(r)
    for k in range(1, hops):
        for r in range(n_parts):
            ring2.step(r, k)
            if (k, r) == (max(hops - 2, 1), 3):
                ow_fourth()
    ow_last()
    mix()
    for r in range(n_parts):
        ring2.step(r, hops)
        finish(r)

    for cp in sent:
        cp.wait_send()
    for i in range(2):
        arrived(w_all.at[0 : quarter * ds, wide : 2 * wide], w_send.at[i])
        arrived(proj_s.at[0 : peers - 1, i], a2a_send.at[1 + i])
    arrived(spec_s.at[0 : ns - 1], a2a_send.at[0])
    arrived(gate_s.at[0 : peers - 1], a2a_send.at[3])
    legs = ow.at[0 : nz - 1, 0, row, sides[0][1]] if plan.x_hi == 2 else ow.at[0 : nz - 1, 0, row, :]
    arrived(legs, ow_send.at[0])
    for r in range(n_parts):
        arrived(own_rows(xl, r), load_sem.at[18 + r])
        arrived(own_rows(other, r), out_recv.at[r])


def make(plan):
    consts = tables(plan)

    def shards(tokens, in_weight, conv_weight, spectrum, skip, out_weight):
        ns, peers, cpd = plan.ns, 2 * plan.ns, plan.cpd
        hops = plan.nz // 2
        vm = pltpu.VMEM
        dma = pltpu.SemaphoreType.DMA
        anywhere = pl.BlockSpec(memory_space=pl.ANY)
        scalars = pl.BlockSpec(memory_space=pltpu.SMEM)
        return pl.pallas_call(
            lambda *refs: kernel(plan, *refs),
            out_shape=jax.ShapeDtypeStruct((plan.tok, plan.ec), BF16),
            in_specs=[anywhere] * 10 + [scalars] * 2,
            out_specs=anywhere,
            scratch_shapes=[
                vm((plan.d, 6 * cpd), BF16),
                vm((plan.half, plan.d), BF16),
                vm((plan.half // 2, 6 * cpd), F32),
                vm((2, 2, cpd, plan.k2), F32), vm((plan.k2, plan.k2), BF16),
                vm((ns, 2, plan.m, 16, LANES), BF16), vm((ns, 2, plan.m, 16, LANES), BF16),
                vm((2, plan.m * ns * 16, LANES), F32),
                vm((peers, 2, 3, 16, LANES), BF16), vm((peers, 2, 3, 16, LANES), BF16),
                vm((3, plan.nhi * SUB, LANES), F32),
                vm((plan.nhi * SUB, LANES), F32),
                vm((peers, plan.rows, LANES), BF16), vm((peers, plan.rows, LANES), BF16),
                vm((plan.half, plan.nch * cpd), BF16),
                vm((plan.nz, 2, cpd, 2 * plan.ec), BF16),
                vm((plan.half, 2 * plan.ec), F32),
                vm((plan.half, plan.ec), BF16), vm((plan.half, plan.ec), BF16),
                vm((2 * plan.ka, plan.nhi), BF16), vm((plan.nhi, 2 * plan.ka), BF16),
                vm((2, plan.ka, LANES), F32),
                vm((2 * LANES, 2 * LANES), BF16), vm((2 * LANES, 2 * LANES), BF16),
                dma((22,)), dma((2, 2, 2, hops)), dma((2, 2, 2, hops)), dma((4, 2, 2, hops)), dma((4, 2, 2, hops)),
                dma((2,)), dma((2,)), dma((3,)), dma((3,)), dma((4,)), dma((4,)),
                dma((plan.n_y + 4,)), dma((plan.n_y + 4,)), dma((4,)), dma((4,)),
            ],
            compiler_params=pltpu.CompilerParams(
                collective_id=0, has_side_effects=True, vmem_limit_bytes=56 * 1024 * 1024
            ),
            name="hyena",
        )(tokens, in_weight, spectrum, out_weight, *consts, conv_weight, skip)

    return shards


def on_mesh(mesh, plan):
    placed = (
        P("seq", "chan"),
        P(None, None, "chan"),
        P(None, None, "chan"),
        P(None, "chan", "seq", None),
        P("chan"),
        P("chan", None),
    )
    return jax.shard_map(make(plan), mesh=mesh, in_specs=placed, out_specs=P("seq", "chan"), check_vma=False)


def solution(mesh):
    return on_mesh(mesh, Plan(ns=16, nch=16, n_y=4, x_hi=2, tok=1024, ds=256, ec=256))
```

```python
import math

import jax
import jax.numpy as jnp
import numpy as np
from jax import lax
from jax.experimental import pallas as pl
from jax.experimental.pallas import tpu as pltpu
from jax.sharding import PartitionSpec as P

MESH = pl.DeviceIdType.MESH
LANES = 128
SUB = 8
BF16 = jnp.bfloat16
F32 = jnp.float32


class Plan:
    def __init__(self, ns, nch, n_y, x_hi, tok, ds, ec):
        self.ns, self.nch, self.nz, self.n_y, self.x_hi = ns, nch, nch // 2, n_y, x_hi
        self.tok, self.half, self.ds, self.ec = tok, tok // 2, ds, ec
        self.cpd = SUB * ns
        self.d, self.e = nch * ds, nch * ec
        self.nhi = ns * tok // LANES
        self.ka = 2 * self.nhi
        self.nfft = 2 * ns * tok
        self.k1 = 2 * ns
        self.m = self.ka // self.k1
        self.k2 = self.m * LANES
        self.blocks = self.half // LANES
        self.rows = self.blocks * SUB
        self.piece = self.cpd // (2 * n_y)


def tables(plan):
    m, s, k1l = np.meshgrid(np.arange(plan.m), np.arange(plan.ns), np.arange(2), indexing="ij")
    ka = (2 * s + k1l + plan.k1 * m).reshape(-1).astype(np.int64)
    nhi = np.arange(plan.nhi, dtype=np.int64)
    lane = np.arange(LANES, dtype=np.int64)

    def angle(a, b, mod):
        return (a[:, None] * b[None, :] % mod) * (2.0 * math.pi / mod)

    left = angle(ka, nhi, plan.ka)
    f1 = np.concatenate([np.cos(left), -np.sin(left)], axis=0)
    g1 = np.concatenate([np.cos(left.T), -np.sin(left.T)], axis=1) / plan.nfft
    turn = angle(ka, lane, plan.nfft)
    tw = np.stack([np.cos(turn), -np.sin(turn)])
    right = angle(lane, lane, LANES)
    c, sn = np.cos(right), np.sin(right)
    f2 = np.block([[c, -sn], [sn, c]])
    g2 = np.block([[c, sn], [-sn, c]])
    order = np.zeros((plan.k2, plan.k2), np.float32)
    k2 = np.arange(plan.k2)
    order[k2, (k2 % plan.m) * LANES + k2 // plan.m] = 1.0
    as_bf16 = lambda a: jnp.asarray(a.astype(np.float32).astype(BF16))
    return (as_bf16(f1), as_bf16(g1), jnp.asarray(tw.astype(np.float32)), as_bf16(f2), as_bf16(g2), as_bf16(order))


def kernel(
    plan, tokens, in_w, spec, out_w, f1_h, g1_h, tw_h, f2_h, g2_h, ord_h, conv_w, skip_w, out,
    w_all, tok_v, acc, spec_v, ord_v, spec_s, spec_r, spec_f, proj_s, proj_r, proj_f,
    gate_f, gate_s, gate_r, gate_a, ow, o_acc, o_own, o_far, f1, g1, tw, f2, g2,
    load_sem, ring_send, ring_recv, ring2_send, ring2_recv, x_send, x_recv, w_send, w_recv,
    a2a_send, a2a_recv, ow_send, ow_recv, out_send, out_recv,
):
    ns, nz, nch, n_y, half, ds, ec, cpd = plan.ns, plan.nz, plan.nch, plan.n_y, plan.half, plan.ds, plan.ec, plan.cpd
    s, c = lax.axis_index("seq"), lax.axis_index("chan")
    core, xh, y = lax.rem(s, 2), lax.rem(s // 2, plan.x_hi), s // (2 * plan.x_hi)
    xl, z = c // nz, lax.rem(c, nz)
    other = 1 - xl
    partner = other * nz + z
    me, here, peers = xl * ns + s, 2 * s + xl, 2 * ns
    hops = nz // 2
    part = half // 2
    wide = 3 * cpd

    def seq_of(y_, xh_, core_):
        return (y_ * plan.x_hi + xh_) * 2 + core_

    def remote(src, dst, ss, rs, seq, chan):
        return pltpu.make_async_remote_copy(
            src_ref=src, dst_ref=dst, send_sem=ss, recv_sem=rs,
            device_id={"seq": seq, "chan": chan}, device_id_type=MESH,
        )

    def arrived(ref, sem):
        pltpu.make_async_copy(ref, ref, sem).wait()

    def place(grp, off):
        k = min(off, nz - off) if isinstance(off, int) else jnp.minimum(off, nz - off)
        return 4 * k - 2 + 2 * ((nz - 1 - off) // hops) + grp

    def origin(side, at):
        grp, off = next((g, o) for g in range(2) for o in range(nz) if place(g, o) == at)
        return (side if grp == 0 else 1 - side) * nz + lax.rem(z + off, nz)

    def rows_of(block):
        return pl.ds(pl.multiple_of(block * ds, ds), ds)

    def start_weights():
        for at in range(nch):
            rows = rows_of(origin(xl, at))
            for p in range(3):
                pltpu.make_async_copy(
                    in_w.at[p, rows, :], w_all.at[at * ds : (at + 1) * ds, p * cpd : (p + 1) * cpd], load_sem.at[1]
                ).start()

    loads = [pltpu.make_async_copy(tokens.at[pl.ds(xl * half, half), :], tok_v.at[:, 0:ds], load_sem.at[0])]
    loads += [pltpu.make_async_copy(a, b, load_sem.at[2 + i]) for i, (a, b) in enumerate(
        [(ord_h, ord_v), (f1_h, f1), (g1_h, g1), (tw_h, tw), (f2_h, f2), (g2_h, g2)])]
    spec_loads = [
        pltpu.make_async_copy(spec.at[p, :, k, :], spec_v.at[p, k], load_sem.at[8 + 2 * p + k])
        for p in range(2) for k in range(2)
    ]

    def hop(by, size):
        return min(by, size - by)

    others = [(dy, dh, dl, dk) for dy in range(n_y) for dh in range(plan.x_hi) for dl in range(2) for dk in range(2)]
    others = sorted(others[1:], key=lambda o: -hop(o[0], n_y) - (2 if o[1] and not o[2] else int(bool(o[1] or o[2]))))

    def peer(o):
        dy, dh, dl, dk = o
        seq = seq_of(lax.rem(y + dy, n_y), lax.rem(xh + dh, plan.x_hi), lax.rem(core + dk, 2))
        return seq, xl if dl == 0 else other

    bar = pltpu.get_barrier_semaphore()

    for dz in range(1, nz):
        there = xl * nz + lax.rem(z + dz, nz)
        pl.semaphore_signal(bar, inc=1, device_id={"seq": s, "chan": there}, device_id_type=MESH)
    for o in reversed(others):
        seq, side = peer(o)
        pl.semaphore_signal(bar, inc=1, device_id={"seq": seq, "chan": side * nz + z}, device_id_type=MESH)
    for cp in loads[:2] + spec_loads:
        cp.start()
    start_weights()
    for cp in loads[2:]:
        cp.start()
    pl.semaphore_wait(bar, peers - 1 + nz - 1)

    reach = {(0, 0): hops, (1, 0): nz - 1 - hops, (0, 1): nz - 1 - hops, (1, 1): hops}
    sent = []

    def go(cp):
        cp.start()
        sent.append(cp)

    class Ring:
        def __init__(self, buf, width, parts, send, recv):
            self.buf, self.width, self.parts, self.send, self.recv = buf, width, parts, send, recv

        def item(self, r, way, grp, k):
            at = place(grp, (nz - k if way == 0 else k) % nz)
            lo, hi = self.parts[r]
            return self.buf.at[lo:hi, at * self.width : (at + 1) * self.width]

        def hand_on(self, r, way, grp, k, src=None):
            to = lax.rem(z + 1, nz) if way == 0 else lax.rem(z + nz - 1, nz)
            go(remote(
                self.item(r, way, grp, k) if src is None else src, self.item(r, way, grp, k + 1),
                self.send.at[r, way, grp, k], self.recv.at[r, way, grp, k], s, xl * nz + to,
            ))

        def begin(self, r, grp, src=None):
            for way in range(2):
                if reach[way, grp] > 0:
                    self.hand_on(r, way, grp, 0, src)

        def step(self, r, k):
            for grp in range(2):
                for way in range(2):
                    if k <= reach[way, grp]:
                        arrived(self.item(r, way, grp, k), self.recv.at[r, way, grp, k - 1])
                        if k < reach[way, grp]:
                            self.hand_on(r, way, grp, k)

    def token_rows(side, r):
        return tokens.at[pl.ds(pl.multiple_of(side * half + r * part, part), part), :]

    ring = Ring(tok_v, ds, [(0, part), (part, half)], ring_send, ring_recv)
    far_home = tok_v.at[:, ds : 2 * ds]

    def swap(r):
        go(remote(token_rows(other, r), far_home.at[r * part : (r + 1) * part, :], x_send.at[r], x_recv.at[r], s, partner))

    swap(0)
    ring.begin(0, 0, token_rows(xl, 0))
    swap(1)
    ring.begin(1, 0, token_rows(xl, 1))

    quarter = nch // 4

    def far_rows(i):
        q = (2 * core + i) * quarter * ds
        return pl.ds(pl.multiple_of(q, quarter * ds), quarter * ds)

    for i, xh_ in ((0, lax.rem(xh + xl, plan.x_hi)), (1, lax.rem(xh + plan.x_hi - 1 + xl, plan.x_hi))):
        for j in range(quarter):
            first, second = origin(other, i * quarter + j), origin(other, (2 + i) * quarter + j)
            rows = rows_of(first + core * (second - first))
            to = pl.ds(pl.multiple_of((2 * core + i) * quarter * ds + j * ds, ds), ds)
            for p in range(3):
                remote(
                    in_w.at[p, rows, :], w_all.at[to, wide + p * cpd : wide + (p + 1) * cpd],
                    w_send.at[i], w_recv.at[i], seq_of(y, xh_, core), partner,
                ).start()

    row = pl.ds(pl.multiple_of((core * n_y + y) * plan.piece, plan.piece), plan.piece)
    if plan.x_hi == 2:
        sides = [(xh, pl.ds(pl.multiple_of(xh * ec, ec), ec))]
    else:
        sides = [(0, pl.ds(0, ec)), (1, pl.ds(ec, ec))]

    def out_cols(g, zz):
        return pl.ds(pl.multiple_of((g * nz + zz) * ec, ec), ec)

    def ow_first(d, carry):
        zz = lax.rem(z + d, nz)
        at = place(0, nz - d) // 2
        for g, to in sides:
            remote(out_w.at[row, out_cols(g, zz)], ow.at[at, 0, row, to], ow_send.at[0], ow_recv.at[0], s, xl * nz + zz).start()
        return carry

    lax.fori_loop(1, nz, ow_first, 0)
    ow_own = [
        pltpu.make_async_copy(out_w.at[row, out_cols(g, z)], ow.at[0, 0, row, to], load_sem.at[12 + i])
        for i, (g, to) in enumerate(sides)
    ]
    for cp in ow_own:
        cp.start()

    arrived(far_home.at[0:part, :], x_recv.at[0])
    ring.begin(0, 1)

    loads[1].wait()
    for p in range(2):
        turned = []
        for k in range(2):
            spec_loads[2 * p + k].wait()
            turned.append(jnp.dot(spec_v[p, k].astype(BF16), ord_v[...], preferred_element_type=F32))
        for m in range(plan.m):
            pair = [t[:, m * LANES : (m + 1) * LANES].reshape(ns, SUB, LANES) for t in turned]
            spec_s[:, p, m] = jnp.concatenate(pair, axis=1).astype(BF16)
    spec_own = pltpu.make_async_copy(spec_s.at[s], spec_r.at[s], load_sem.at[14])
    spec_own.start()

    def send_spec(d, carry):
        q = lax.rem(s + d, ns)
        remote(spec_s.at[q], spec_r.at[s], a2a_send.at[0], a2a_recv.at[0], q, c).start()
        return carry

    lax.fori_loop(1, ns, send_spec, 0)

    def pack(value, r, g, p):
        pair = [value[i * LANES : (i + 1) * LANES, :].T.reshape(ns, SUB, LANES) for i in range(2)]
        at = xl if g == 0 else other
        proj_s[pl.ds(at * ns, ns), r, p] = jnp.concatenate(pair, axis=1).astype(BF16)

    def send_proj(r, g):
        for o in others:
            seq, side = peer(o)
            if o[2] == g:
                remote(
                    proj_s.at[side * ns + seq, r], proj_r.at[here, r], a2a_send.at[1 + r], a2a_recv.at[1 + r],
                    seq, side * nz + z,
                ).start()
        if g == 0:
            pltpu.make_async_copy(proj_s.at[me, r], proj_r.at[here, r], load_sem.at[15 + r]).start()

    def project(r, g):
        rows = slice(r * part, (r + 1) * part)
        value = jnp.dot(tok_v[rows, :], w_all[:, g * wide : (g + 1) * wide], preferred_element_type=F32)
        for p in range(3):
            pack(value[:, p * cpd : (p + 1) * cpd], r, g, p)
        send_proj(r, g)

    def ow_second():
        for cp in ow_own:
            cp.wait()
        mine = ow.at[:, 0, row, sides[0][1]] if plan.x_hi == 2 else ow.at[:, 0, row, :]
        arrived(mine.at[0 : nz - 1], ow_recv.at[0])
        far = ow.at[:, 1, row, sides[0][1]] if plan.x_hi == 2 else ow.at[:, 1, row, :]
        go(remote(mine, far, ow_send.at[1], ow_recv.at[1], s, partner))
        if plan.x_hi == 2:
            go(remote(mine, mine, ow_send.at[2], ow_recv.at[2], seq_of(y, 1 - xh, core), c))
            go(remote(mine, far, ow_send.at[3], ow_recv.at[3], seq_of(y, 1 - xh, core), partner))

    def ow_third():
        if plan.x_hi == 2:
            away = pl.ds(pl.multiple_of((1 - xh) * ec, ec), ec)
            arrived(ow.at[:, 1, row, sides[0][1]], ow_recv.at[1])
            arrived(ow.at[:, 0, row, away], ow_recv.at[2])
            arrived(ow.at[:, 1, row, away], ow_recv.at[3])
        else:
            arrived(ow.at[:, 1, row, :], ow_recv.at[1])
        for dy in range(1, n_y):
            go(remote(ow.at[:, :, row, :], ow.at[:, :, row, :], ow_send.at[3 + dy], ow_recv.at[3 + dy],
                      seq_of(lax.rem(y + dy, n_y), xh, core), c))

    half_ow = n_y * plan.piece

    def ow_fourth():
        for dy in range(1, n_y):
            yy = lax.rem(y + n_y - dy, n_y)
            piece = pl.ds(pl.multiple_of((core * n_y + yy) * plan.piece, plan.piece), plan.piece)
            arrived(ow.at[:, :, piece, :], ow_recv.at[3 + dy])
        side = pl.ds(pl.multiple_of(core * half_ow, half_ow), half_ow)
        go(remote(ow.at[:, :, side, :], ow.at[:, :, side, :], ow_send.at[3 + n_y], ow_recv.at[3 + n_y], seq_of(y, xh, 1 - core), c))

    def ow_last():
        away = pl.ds(pl.multiple_of((1 - core) * half_ow, half_ow), half_ow)
        arrived(ow.at[:, :, away, :], ow_recv.at[3 + n_y])

    def far_pass():
        for i in range(2):
            arrived(w_all.at[far_rows(i), wide : 2 * wide], w_recv.at[i])
        side = pl.ds(pl.multiple_of(core * 2 * quarter * ds, 2 * quarter * ds), 2 * quarter * ds)
        mine = w_all.at[side, wide : 2 * wide]
        go(remote(mine, mine, w_send.at[2], w_recv.at[2], seq_of(y, xh, 1 - core), c))

    def far_wait():
        away = pl.ds(pl.multiple_of((1 - core) * 2 * quarter * ds, 2 * quarter * ds), 2 * quarter * ds)
        arrived(w_all.at[away, wide : 2 * wide], w_recv.at[2])

    def own_wait():
        loads[0].wait()
        arrived(w_all.at[:, 0:wide], load_sem.at[1])

    def begin_second():
        arrived(far_home.at[part : 2 * part, :], x_recv.at[1])
        ring.begin(1, 1)

    bulk = (nch - 2) * ds
    rows = slice(part, 2 * part)

    def bulk_second():
        for at in range(0, 2 * wide, 2 * cpd):
            acc[:, at : at + 2 * cpd] = jnp.dot(
                tok_v[rows, 0:bulk], w_all[0:bulk, at : at + 2 * cpd], preferred_element_type=F32)

    after = {}
    steps = sorted((k + r * (hops - 1.5), r, k) for r in range(2) for k in range(1, hops + 1))
    place_of = {(r, k): i for i, (_, r, k) in enumerate(steps)}

    def hook(r, k, *does):
        k = max(1, min(k, hops))
        after.setdefault(place_of[r, k], []).extend(does)

    hook(0, 2, begin_second)
    hook(1, 1, ow_second)
    hook(0, hops, own_wait, lambda: project(0, 0))
    hook(1, 2, far_pass)
    hook(1, hops - 1, far_wait, lambda: project(0, 1), bulk_second)
    for i, (_, r, k) in enumerate(steps):
        ring.step(r, k)
        for do in after.get(i, []):
            do()
    for g in range(2):
        half_of = slice(g * wide, (g + 1) * wide)
        rest = acc[:, half_of] + jnp.dot(tok_v[rows, bulk:], w_all[bulk:, half_of], preferred_element_type=F32)
        for p in range(3):
            pack(rest[:, p * cpd : (p + 1) * cpd], 1, g, p)
        send_proj(1, g)

    spec_own.wait()
    arrived(spec_r.at[0 : ns - 1], a2a_recv.at[0])

    def lay(i, carry):
        for p in range(2):
            for m in range(plan.m):
                spec_f[p, pl.ds(pl.multiple_of((m * ns + i) * 16, 16), 16), :] = spec_r[i, p, m].astype(F32)
        return carry

    lax.fori_loop(0, ns, lay, 0)
    for cp in loads[2:]:
        cp.wait()
    for r in range(2):
        arrived(proj_r.at[here, r], load_sem.at[15 + r])
        arrived(proj_r.at[0 : peers - 1, r], a2a_recv.at[1 + r])
        for p in range(3):
            for q in range(peers):
                proj_f[p, q * plan.rows + 16 * r : q * plan.rows + 16 * (r + 1), :] = proj_r[q, r, p].astype(F32)

    lane = lax.broadcasted_iota(jnp.int32, (plan.nhi, LANES), 1)
    posn = lane + LANES * lax.broadcasted_iota(jnp.int32, (plan.nhi, LANES), 0)

    def behind(x, by):
        turned = pltpu.roll(x, by, 1)
        both = jnp.where(lane < by, pltpu.roll(turned, 1, 0), turned)
        return jnp.where(posn < by, 0.0, both)

    def streams(ch):
        parts = []
        for p in range(3):
            x = proj_f[p, pl.ds(ch, plan.nhi, stride=SUB), :]
            f = conv_w[0, p, s * SUB + ch] * x
            for j in range(1, 3):
                f = f + conv_w[j, p, s * SUB + ch] * behind(x, j)
            parts.append(f)
        return parts[0], (parts[1] * parts[2]).astype(BF16)

    def middle(ch, a):
        ar, ai = a[: plan.ka], a[plan.ka :]
        tr, ti = tw[0], tw[1]
        yy = jnp.concatenate([(ar * tr - ai * ti).astype(BF16), (ar * ti + ai * tr).astype(BF16)], axis=1)
        zz = jnp.dot(yy, f2[...], preferred_element_type=F32)
        zr, zi = zz[:, :LANES], zz[:, LANES:]
        hr, hi = (spec_f[p, pl.ds(ch, plan.ka, stride=SUB), :] for p in range(2))
        pp = jnp.concatenate([(zr * hr - zi * hi).astype(BF16), (zr * hi + zi * hr).astype(BF16)], axis=1)
        u = jnp.dot(pp, g2[...], preferred_element_type=F32)
        ur, ui = u[:, :LANES], u[:, LANES:]
        return jnp.concatenate([(ur * tr + ui * ti).astype(BF16), (ui * tr - ur * ti).astype(BF16)], axis=0)

    for ch in range(0, SUB, 2):
        both = [streams(ch + i) for i in range(2)]
        a = jnp.dot(f1[...], jnp.concatenate([signal for _, signal in both], axis=1), preferred_element_type=F32)
        v = jnp.concatenate([middle(ch + i, a[:, i * LANES : (i + 1) * LANES]) for i in range(2)], axis=1)
        longconv = jnp.dot(g1[...], v, preferred_element_type=F32)
        for i, (query, signal) in enumerate(both):
            direct = skip_w[s * SUB + ch + i] * signal.astype(F32)
            gate_f[pl.ds(ch + i, plan.nhi, stride=SUB), :] = query * (longconv[:, i * LANES : (i + 1) * LANES] + direct)

    gate_s[...] = gate_f[...].astype(BF16).reshape(peers, plan.rows, LANES)

    for o in others:
        seq, side = peer(o)
        remote(gate_s.at[2 * seq + side], gate_r.at[me], a2a_send.at[3], a2a_recv.at[3], seq, side * nz + z).start()
    gate_own = pltpu.make_async_copy(gate_s.at[here], gate_r.at[me], load_sem.at[17])
    gate_own.start()
    gate_own.wait()
    arrived(gate_r.at[0 : peers - 1], a2a_recv.at[3])

    n_parts = 4
    parts2 = [(i * half // n_parts, (i + 1) * half // n_parts) for i in range(n_parts)]
    ring2 = Ring(gate_a, cpd, parts2, ring2_send, ring2_recv)

    def repack(r):
        lo, hi = parts2[r]
        for grp in range(2):
            for j in range(lo // LANES, hi // LANES):
                rows = gate_r[pl.ds((xl if grp == 0 else other) * ns, ns), 16 * (j // 2) : 16 * (j // 2 + 1), :].astype(F32)
                block = rows[:, SUB * (j % 2) : SUB * (j % 2 + 1), :].reshape(cpd, LANES)
                gate_a[j * LANES : (j + 1) * LANES, grp * cpd : (grp + 1) * cpd] = block.T.astype(BF16)
            ring2.begin(r, grp)

    k_bulk = (nch - 2) * cpd

    def weights(lo, hi):
        return ow[lo // (2 * cpd) : hi // (2 * cpd)].reshape(hi - lo, 2 * ec)

    def mix():
        o_acc[...] = jnp.dot(gate_a[:, 0:k_bulk], weights(0, k_bulk), preferred_element_type=F32)

    def own_rows(side, r):
        lo, hi = parts2[r]
        return out.at[pl.ds(pl.multiple_of(side * half + lo, LANES), hi - lo), :]

    def finish(r):
        lo, hi = parts2[r]
        total = o_acc[lo:hi, :] + jnp.dot(gate_a[lo:hi, k_bulk:], weights(k_bulk, nch * cpd), preferred_element_type=F32)
        left, right = total[:, :ec].astype(BF16), total[:, ec:].astype(BF16)
        o_far[lo:hi, :] = jnp.where(xl == 0, right, left)
        go(remote(o_far.at[lo:hi, :], own_rows(xl, r), out_send.at[r], out_recv.at[r], s, partner))
        o_own[lo:hi, :] = jnp.where(xl == 0, left, right)
        pltpu.make_async_copy(o_own.at[lo:hi, :], own_rows(xl, r), load_sem.at[18 + r]).start()

    ow_third()
    repack(0)
    for r in range(1, n_parts):
        repack(r)
    for k in range(1, hops):
        for r in range(n_parts):
            ring2.step(r, k)
            if (k, r) == (max(hops - 2, 1), 3):
                ow_fourth()
    ow_last()
    mix()
    for r in range(n_parts):
        ring2.step(r, hops)
        finish(r)

    for cp in sent:
        cp.wait_send()
    for i in range(2):
        arrived(w_all.at[0 : quarter * ds, wide : 2 * wide], w_send.at[i])
        arrived(proj_s.at[0 : peers - 1, i], a2a_send.at[1 + i])
    arrived(spec_s.at[0 : ns - 1], a2a_send.at[0])
    arrived(gate_s.at[0 : peers - 1], a2a_send.at[3])
    legs = ow.at[0 : nz - 1, 0, row, sides[0][1]] if plan.x_hi == 2 else ow.at[0 : nz - 1, 0, row, :]
    arrived(legs, ow_send.at[0])
    for r in range(n_parts):
        arrived(own_rows(xl, r), load_sem.at[18 + r])
        arrived(own_rows(other, r), out_recv.at[r])


def make(plan):
    consts = tables(plan)

    def shards(tokens, in_weight, conv_weight, spectrum, skip, out_weight):
        ns, peers, cpd = plan.ns, 2 * plan.ns, plan.cpd
        hops = plan.nz // 2
        vm = pltpu.VMEM
        dma = pltpu.SemaphoreType.DMA
        anywhere = pl.BlockSpec(memory_space=pl.ANY)
        scalars = pl.BlockSpec(memory_space=pltpu.SMEM)
        return pl.pallas_call(
            lambda *refs: kernel(plan, *refs),
            out_shape=jax.ShapeDtypeStruct((plan.tok, plan.ec), BF16),
            in_specs=[anywhere] * 10 + [scalars] * 2,
            out_specs=anywhere,
            scratch_shapes=[
                vm((plan.d, 6 * cpd), BF16),
                vm((plan.half, plan.d), BF16),
                vm((plan.half // 2, 6 * cpd), F32),
                vm((2, 2, cpd, plan.k2), F32), vm((plan.k2, plan.k2), BF16),
                vm((ns, 2, plan.m, 16, LANES), BF16), vm((ns, 2, plan.m, 16, LANES), BF16),
                vm((2, plan.m * ns * 16, LANES), F32),
                vm((peers, 2, 3, 16, LANES), BF16), vm((peers, 2, 3, 16, LANES), BF16),
                vm((3, plan.nhi * SUB, LANES), F32),
                vm((plan.nhi * SUB, LANES), F32),
                vm((peers, plan.rows, LANES), BF16), vm((peers, plan.rows, LANES), BF16),
                vm((plan.half, plan.nch * cpd), BF16),
                vm((plan.nz, 2, cpd, 2 * plan.ec), BF16),
                vm((plan.half, 2 * plan.ec), F32),
                vm((plan.half, plan.ec), BF16), vm((plan.half, plan.ec), BF16),
                vm((2 * plan.ka, plan.nhi), BF16), vm((plan.nhi, 2 * plan.ka), BF16),
                vm((2, plan.ka, LANES), F32),
                vm((2 * LANES, 2 * LANES), BF16), vm((2 * LANES, 2 * LANES), BF16),
                dma((22,)), dma((2, 2, 2, hops)), dma((2, 2, 2, hops)), dma((4, 2, 2, hops)), dma((4, 2, 2, hops)),
                dma((2,)), dma((2,)), dma((3,)), dma((3,)), dma((4,)), dma((4,)),
                dma((plan.n_y + 4,)), dma((plan.n_y + 4,)), dma((4,)), dma((4,)),
            ],
            compiler_params=pltpu.CompilerParams(
                collective_id=0, has_side_effects=True, vmem_limit_bytes=56 * 1024 * 1024
            ),
            name="hyena",
        )(tokens, in_weight, spectrum, out_weight, *consts, conv_weight, skip)

    return shards


def on_mesh(mesh, plan):
    placed = (
        P("seq", "chan"),
        P(None, None, "chan"),
        P(None, None, "chan"),
        P(None, "chan", "seq", None),
        P("chan"),
        P("chan", None),
    )
    return jax.shard_map(make(plan), mesh=mesh, in_specs=placed, out_specs=P("seq", "chan"), check_vma=False)


def solution(mesh):
    return on_mesh(mesh, Plan(ns=16, nch=16, n_y=4, x_hi=2, tok=1024, ds=256, ec=256))
```
